32 devices in a mesh: sx: 4 (over z), sy: 4 (over y, x), rep: 2 (over core).
Axes of the slice: x: 2, y: 2, z: 4, core: 2. Of those that a mesh axis runs over, the one named last changes fastest.
Arguments:
- volume: bfloat16 [2, 32, 8, 64, 256], P('rep', None, 'sx', 'sy'), may hold values from -6 to 6
- first_kernel: bfloat16 [64, 32, 3, 3, 3], replicated, may hold values from -0.21875 to 0.21875
- first_bias: float32 [64], replicated, may hold values from -3 to 3
- second_kernel: bfloat16 [128, 64, 3, 3, 3], P('sy'), may hold values from -0.15625 to 0.15625
- second_bias: float32 [128], P('sy'), may hold values from -3 to 3
- cotangent: bfloat16 [2, 128, 4, 32, 128], P('rep', 'sy', 'sx'), may hold values from -6 to 6
Outputs:
- second_out: float32 [2, 128, 4, 32, 128], P('rep', 'sy', 'sx')
- grad_first_kernel: float32 [64, 32, 3, 3, 3], replicated
- grad_first_bias: float32 [64], replicated
- grad_second_kernel: float32 [128, 64, 3, 3, 3], P('sy')
- grad_second_bias: float32 [128], P('sy')
The draws below stay inside these ranges and needn't reach their ends.
All inputs are finite; a program needn't handle non-finite values.
Results may differ from the reference program's by a relative error of at most 0.0045.
Values may be sent and summed in bfloat16 or wider, within the bound.
No kernel may reach another device: no remote copies, remote signals or barrier semaphores. Data moves between devices by JAX's collectives and lax.ppermute only.
A program may use at most 128 MiB of HBM per device.

```python
import jax
import jax.numpy as jnp
from jax import lax

CIN = 32
C1 = 64
C2 = 128
CZ = 256
BATCH = 2
NX = 8
NY = 64
NX2 = 4
NY2 = 32
CZ2 = 128


def block_levels(stream_key, dims, cuts, smallest, top_value):
    def one(position, shards_of):
        steps = jax.random.uniform(jax.random.fold_in(jax.random.fold_in(stream_key, 6), position), (shards_of,), jnp.float32, smallest / len(cuts), top_value / len(cuts))
        return jnp.repeat(jnp.exp(steps), dims[position] // shards_of).reshape((-1,) + (1,) * (len(dims) - position - 1))

    factor_of = one(*cuts[0])
    for cut in cuts[1:]:
        factor_of = factor_of * one(*cut)
    return factor_of


def scatter_about(stream_key, extent, scale, bound, cuts=(), held_as=jnp.bfloat16):
    factor_of = block_levels(stream_key, extent, cuts, -0.22, 0.18) if cuts else 1.0
    entries = jax.random.normal(stream_key, extent, jnp.float32) * scale * factor_of
    return jnp.minimum(jnp.maximum(entries, -bound), bound).astype(held_as)


def setup_inputs(seed: int = 0) -> dict:
    streams_of = jax.random.split(jax.random.key(seed), 7)
    return {
        "volume": scatter_about(streams_of[0], (BATCH, CIN, NX, NY, CZ), 1.0, 6.0, ((0, 2), (2, 4), (3, 4))),
        "first_kernel": scatter_about(streams_of[1], (C1, CIN, 3, 3, 3), (CIN * 27) ** -0.5, 0.21875),
        "first_bias": scatter_about(streams_of[2], (C1,), 0.5, 3.0, (), jnp.float32),
        "second_kernel": scatter_about(streams_of[3], (C2, C1, 3, 3, 3), (C1 * 27) ** -0.5, 0.15625, ((0, 4),)),
        "second_bias": scatter_about(streams_of[4], (C2,), 0.5, 3.0, ((0, 4),), jnp.float32),
        "cotangent": scatter_about(streams_of[5], (BATCH, C2, NX2, NY2, CZ2), 1.0, 6.0, ((0, 2), (1, 4), (2, 4))),
    }


def convolve(field, kernel):
    return lax.conv_general_dilated(field[None], kernel, (1, 1, 1), 'SAME', dimension_numbers=('NCDHW', 'OIDHW', 'NCDHW'), preferred_element_type=jnp.float32)[0]

def weight_terms(cotan, source):
    cells_x, cells_y, cells_z = (cotan.shape[1], cotan.shape[2], cotan.shape[3])
    padded = jnp.pad(source.astype(jnp.float32), ((0, 0), (1, 1), (1, 1), (1, 1)))
    grads = cotan.astype(jnp.float32)
    terms = []
    for i in range(3):
        for j in range(3):
            for k in range(3):
                piece = padded[:, i:i + cells_x, j:j + cells_y, k:k + cells_z]
                terms.append(jnp.einsum('oxyz,cxyz->oc', grads, piece, precision=lax.Precision.HIGHEST))
    stacked = jnp.stack(terms).reshape(3, 3, 3, grads.shape[0], source.shape[0])
    return stacked.transpose(3, 4, 0, 1, 2)

def pool_mean(field):
    chans, cells_x, cells_y, cells_z = field.shape
    blocks = field.astype(jnp.float32).reshape(chans, cells_x // 2, 2, cells_y // 2, 2, cells_z // 2, 2)
    return lax.optimization_barrier(jnp.mean(blocks, axis=(2, 4, 6)))

def reference(volume, first_kernel, first_bias, second_kernel, second_bias, cotangent):
    scale = 1.0 / jnp.sqrt(jnp.float32(BATCH * NX2 * NY2 * CZ2))
    flipped = second_kernel.transpose(1, 0, 2, 3, 4)[:, :, ::-1, ::-1, ::-1]
    outs = []
    grad_w1 = jnp.zeros((C1, CIN, 3, 3, 3), jnp.float32)
    grad_b1 = jnp.zeros((C1,), jnp.float32)
    grad_w2 = jnp.zeros((C2, C1, 3, 3, 3), jnp.float32)
    grad_b2 = jnp.zeros((C2,), jnp.float32)
    for sample in range(BATCH):
        source = volume[sample]
        pre = convolve(source, first_kernel) + first_bias[:, None, None, None]
        act = jnp.where(pre > 0, pre, 0.3 * pre)
        pooled = pool_mean(act).astype(jnp.bfloat16)
        second = convolve(pooled, second_kernel) + second_bias[:, None, None, None]
        outs.append(second.astype(jnp.float32))
        cotan = cotangent[sample]
        grad_w2 = grad_w2 + weight_terms(cotan, pooled)
        grad_b2 = grad_b2 + lax.optimization_barrier(jnp.sum(cotan.astype(jnp.float32), axis=(1, 2, 3)))
        back = convolve(cotan, flipped)
        spread = jnp.repeat(jnp.repeat(jnp.repeat(back, 2, axis=1), 2, axis=2), 2, axis=3)
        grad_pre = (spread * 0.125 * jnp.where(pre > 0, 1.0, 0.3)).astype(jnp.bfloat16)
        grad_w1 = grad_w1 + weight_terms(grad_pre, source)
        grad_b1 = grad_b1 + lax.optimization_barrier(jnp.sum(grad_pre.astype(jnp.float32), axis=(1, 2, 3)))
    second_out = jnp.stack(outs)
    return (second_out, scale * grad_w1, scale * grad_b1, scale * grad_w2, scale * grad_b2)
```

```python
import functools
import math

import jax
import jax.numpy as jnp
from jax import lax
from jax.experimental import pallas as pl
from jax.experimental.pallas import tpu as pltpu
from jax.sharding import PartitionSpec as P

BF = jnp.bfloat16
F32 = jnp.float32
VMEM_BYTES = 48 * 1024 * 1024


def dot(a, b):
    return jnp.dot(a, b, preferred_element_type=F32)


def dot_nt(a, b):
    return lax.dot_general(a, b, (((1,), (1,)), ((), ())), preferred_element_type=F32)


def index_pair(rows, cols):
    shape = (rows, cols)
    return (
        lax.broadcasted_iota(jnp.int32, shape, 0),
        lax.broadcasted_iota(jnp.int32, shape, 1),
    )


def one_where(cond):
    return jnp.where(cond, 1.0, 0.0).astype(BF)


def swap_majors(outer, inner):
    r, c = index_pair(outer * inner, outer * inner)
    return one_where(lax.rem(r, outer) * inner + lax.div(r, outer) == c)


def shift_both(width):
    r, c = index_pair(width, 2 * width)
    return one_where(((c < width) & (r == c - 1)) | ((c >= width) & (r == c - width + 1)))


def identity(size):
    r, c = index_pair(size, size)
    return one_where(r == c)


def call(body, name, outs, scratch, ins, smem_ins=0, flops=0):
    vm = pl.BlockSpec(memory_space=pltpu.VMEM)
    sm = pl.BlockSpec(memory_space=pltpu.SMEM)
    return pl.pallas_call(
        body,
        name=name,
        out_shape=outs,
        in_specs=[sm] * smem_ins + [vm] * (len(ins) - smem_ins),
        out_specs=jax.tree.map(lambda _: vm, outs),
        scratch_shapes=scratch,
        compiler_params=pltpu.CompilerParams(vmem_limit_bytes=VMEM_BYTES),
        cost_estimate=pl.CostEstimate(flops=flops, bytes_accessed=1 << 20, transcendentals=0),
    )(*ins)


def prep_body(me, vol, cot, vt, cp, cpad):
    cin, planes, rows, width = vol.shape
    swap = swap_majors(cin, rows)
    half = width // 2
    r, c = index_pair(width, width)
    split = one_where(r == 2 * lax.rem(c, half) + lax.div(c, half))
    for x in range(planes):
        cells = dot(swap, vol[:, x].reshape(cin * rows, width)).astype(BF)
        vt[x] = dot(cells, split).astype(BF).reshape(rows, cin, width)
    nf, rows2, width2 = cot.shape
    step = 16
    swap2 = swap if nf == cin and rows == step else swap_majors(nf, step)
    for h in range(0, rows2, step):
        got = dot(swap2, cot[:, h : h + step].reshape(nf * step, width2))
        cpad[1 + h : 1 + h + step] = got.astype(BF).reshape(step, nf, width2)
    zero = jnp.zeros((1, nf, width2), BF)
    cpad[0:1] = zero
    cpad[rows2 + 1 : rows2 + 2] = zero
    count, rim_rows = cp.shape[0], cp.shape[1]
    for s in range(count):
        cp[s] = cpad[pl.ds((me[0] ^ s) * (rim_rows - 2), rim_rows)]


def conv1_body(odd, vr, za, zb, w1q, bias, cells, mask, pooled, w1b):
    planes, rows, cin, width = vr.shape
    half = width // 2
    c1 = bias.shape[0] // 4
    eye = identity(4 * c1)
    nothing = jnp.zeros((cin, 2 * c1), BF)
    for i in range(3):
        blocks = []
        for ys in range(4):
            for slot in range(4):
                left = w1q[i, ys, slot] if ys < 3 else nothing
                right = w1q[i, ys - 1, slot] if ys > 0 else nothing
                blocks.append(jnp.concatenate([left, right], axis=1))
        w1b[i] = dot_nt(eye, jnp.concatenate(blocks, axis=0)).astype(BF)
    r, c = index_pair(width, width)
    moved = one_where(
        ((c < half) & (c > 0) & (r == half + c - 1)) | ((c >= half) & (r == c - half + 1) & (r < half))
    )
    is_odd = odd[0] == 1
    for x in range(planes + 2):
        if x == 0:
            plane = jnp.where(is_odd, za[...], zb[...])
        elif x == planes + 1:
            plane = jnp.where(is_odd, zb[...], za[...])
        else:
            plane = vr[x - 1]
        out = dot(plane.reshape(rows * cin, width), moved).astype(BF).reshape(rows, cin, width)
        cells[x, :, 0:cin] = out[:, :, :half]
        cells[x, :, cin : 2 * cin] = plane[:, :, :half]
        cells[x, :, 2 * cin : 3 * cin] = plane[:, :, half:]
        cells[x, :, 3 * cin : 4 * cin] = out[:, :, half:]
    pairs = pooled.shape[0] // 2
    deep = 16 * cin
    for t in range(pairs):
        total = None
        for xp in range(2):
            acc = None
            for i in range(3):
                rhs = jnp.concatenate(
                    [
                        cells[xp + i, 4 * t : 4 * t + 4].reshape(deep, half),
                        cells[xp + i, 4 * t + 2 : 4 * t + 6].reshape(deep, half),
                    ],
                    axis=1,
                )
                part = dot(w1b[i], rhs)
                acc = part if acc is None else acc + part
            pre = acc + bias[...]
            above = pre > 0
            mask[xp, t] = jnp.where(above, 1.0, 0.0).astype(BF)
            act = jnp.where(above, pre, 0.3 * pre)
            for b in range(4):
                piece = act[b * c1 : (b + 1) * c1]
                total = piece if total is None else total + piece
        mean = (total * 0.125).astype(BF)
        pooled[2 * t] = mean[:, :half]
        pooled[2 * t + 1] = mean[:, half:]


def with_shifts(store, plane, shifts):
    rows, chans, width = plane.shape
    out = dot(plane.reshape(rows * chans, width), shifts).astype(BF).reshape(rows, chans, 2 * width)
    store(0, out[:, :, :width])
    store(1, plane)
    store(2, out[:, :, width:])


def conv2_body(odd, ur, ua, ub, w2r, pieces, u):
    rows, c1, width = ur.shape
    count, pairs, nf, _ = w2r.shape
    shifts = shift_both(width)
    is_odd = odd[0] == 1
    planes = (
        jnp.where(is_odd, ua[...], ub[...]),
        ur[...],
        jnp.where(is_odd, ub[...], ua[...]),
    )
    for x in range(3):

        def store(k, value, x=x):
            u[x, :, k] = value

        with_shifts(store, planes[x], shifts)
    weights = jnp.concatenate(
        [jnp.concatenate([w2r[s, p] for s in range(count)], axis=0) for p in range(pairs)], axis=1
    )

    def tap(y, d):
        d = d if d < 27 else 0
        return u[d // 9, y + (d // 3) % 3, d % 3]

    def deep(y):
        return jnp.concatenate(
            [tap(y, d) for p in range(pairs) for d in (p, p + pairs)], axis=0
        )

    for y in range(0, rows - 2, 2):
        rhs = jnp.concatenate([deep(y), deep(y + 1)], axis=1)
        out = dot(weights, rhs).astype(BF)
        for s in range(count):
            pieces[s, y] = out[s * nf : (s + 1) * nf, :width]
            pieces[s, y + 1] = out[s * nf : (s + 1) * nf, width:]


def back_body(odd, cells, mask, pooled, co, ca, cb, w2r, red, t_ref, wb, gp, g2):
    count, rows, nf, width = co.shape
    pairs = w2r.shape[1]
    c1 = pooled.shape[1]
    c2 = count * nf
    cin = cells.shape[2] // 4
    shifts = shift_both(width)
    is_odd = odd[0] == 1
    for x in range(3):
        for s in range(count):
            if x == 1:
                plane = co[s]
            elif x == 0:
                plane = jnp.where(is_odd, ca[s], cb[s])
            else:
                plane = jnp.where(is_odd, cb[s], ca[s])

            def store(k, value, x=x, s=s):
                t_ref[x, :, k, s * nf : (s + 1) * nf] = value

            with_shifts(store, plane, shifts)
    eye = identity(2 * c1)
    for p in range(pairs):
        block = jnp.concatenate([w2r[s, p] for s in range(count)], axis=0)
        turned = dot_nt(eye, block)
        for half, d in ((0, p), (1, p + pairs)):
            if d < 27:
                i, j, k = d // 9, (d // 3) % 3, d % 3
                at = ((2 - j) * 3 + (2 - k)) * c2
                wb[2 - i, :, at : at + c2] = turned[half * c1 : (half + 1) * c1].astype(BF)
    deep = 9 * c2
    bias1 = jnp.zeros((8, 4 * c1), F32)
    ones = jnp.ones((8, 2 * width), BF)
    for t in range((rows - 2) // 2):
        acc = None
        for x in range(3):
            rhs = jnp.concatenate(
                [
                    t_ref[x, 2 * t : 2 * t + 3].reshape(deep, width),
                    t_ref[x, 2 * t + 1 : 2 * t + 4].reshape(deep, width),
                ],
                axis=1,
            )
            part = dot(wb[x], rhs)
            acc = part if acc is None else acc + part
        eighth = acc * 0.125
        spread = jnp.concatenate([eighth] * 4, axis=0)
        for xp in range(2):
            grad = (spread * jnp.where(mask[xp, t] > 0, 1.0, 0.3)).astype(BF)
            gp[xp, t] = grad
            bias1 = bias1 + dot_nt(ones, grad)
    n_pairs = (rows - 2) // 2
    lane = lax.broadcasted_iota(jnp.int32, (cin, 2 * c1), 1)
    low_half = lane < c1
    lows, highs = {}, {}
    for i in range(3):
        acc = None
        for xp in range(2):
            for t in range(n_pairs):
                lhs = jnp.concatenate(
                    [
                        cells[xp + i, 4 * t : 4 * t + 4].reshape(16 * cin, width),
                        cells[xp + i, 4 * t + 2 : 4 * t + 6].reshape(16 * cin, width),
                    ],
                    axis=1,
                )
                part = dot_nt(lhs, gp[xp, t])
                acc = part if acc is None else acc + part
        for j in range(3):
            slots = []
            for slot in range(4):
                r0 = (j * 4 + slot) * cin
                r1 = ((j + 1) * 4 + slot) * cin
                slots.append(acc[r0 : r0 + cin, : 2 * c1] + acc[r1 : r1 + cin, 2 * c1 :])
            turned = [pltpu.roll(v, c1, 1) for v in slots]
            for k in range(3):
                d = (i * 3 + j) * 3 + k
                if d < pairs:
                    lows[d] = slots[k] + turned[k + 1]
                    red[d, c2 : c2 + cin] = lows[d]
                else:
                    high = slots[k + 1] + turned[k]
                    p = d - pairs
                    red[p, c2 : c2 + cin] = jnp.where(low_half, red[p, c2 : c2 + cin], high)
    b1 = bias1[:, : 2 * c1] + bias1[:, 2 * c1 :]
    b1 = b1 + pltpu.roll(b1, c1, 1)
    b1 = jnp.concatenate([b1] * (cin // 8), axis=0)
    red[pairs - 1, c2 : c2 + cin] = jnp.where(low_half, red[pairs - 1, c2 : c2 + cin], b1)
    rhs = jnp.concatenate(
        [jnp.concatenate([pooled[y], pooled[y]], axis=0) for y in range(rows - 2)], axis=1
    )
    low_wide = lax.broadcasted_iota(jnp.int32, (c2, 2 * c1), 1) < c1
    for x in range(3):
        for ys in range(3):
            lhs = jnp.concatenate(
                [t_ref[x, y + ys].reshape(3 * c2, width) for y in range(rows - 2)], axis=1
            )
            out = dot_nt(lhs, rhs)
            for zs in range(3):
                d = ((2 - x) * 3 + (2 - ys)) * 3 + (2 - zs)
                g2[d] = out[zs * c2 : (zs + 1) * c2]
    sums = None
    for y in range(1, rows - 1):
        v = t_ref[1, y, 1].astype(F32)
        sums = v if sums is None else sums + v
    b2 = jnp.broadcast_to(jnp.sum(sums, axis=1, keepdims=True), (c2, 2 * c1))
    for p in range(pairs):
        other = g2[p + pairs] if p + pairs < 27 else b2
        red[p, 0:c2] = jnp.where(low_wide, g2[p], other)


def unpack_body(me, *refs):
    pieces, bias, out = refs[:-2], refs[-2], refs[-1]
    rows, nf, width = pieces[0].shape
    swap = swap_majors(rows, nf)
    for s, piece in enumerate(pieces):
        got = dot(swap, piece[...].reshape(rows * nf, width)).reshape(nf, rows, width)
        out[:, pl.ds(pl.multiple_of((me[0] ^ s) * rows, rows), rows), :] = got + bias[...]


def swap_first(value, axis):
    count = lax.axis_size(axis)
    return lax.ppermute(value, axis, [(i, i ^ 1) for i in range(count)])


def swap_second(value, axis):
    count = lax.axis_size(axis)
    pairs = [(i, i + 1) for i in range(1, count - 1, 2)]
    return lax.ppermute(value, axis, pairs + [(b, a) for a, b in pairs])


def to_partner(value, axis, s):
    count = lax.axis_size(axis)
    return lax.ppermute(value, axis, [(i, i ^ s) for i in range(count)])


def tree_sum(values):
    values = list(values)
    while len(values) > 1:
        values = [values[n] + values[n + 1] for n in range(0, len(values), 2)]
    return values[0]


def per_device(volume, first_kernel, first_bias, second_kernel, second_bias, cotangent):
    source = volume[0]
    cotan = cotangent[0, :, 0]
    n_sy, n_sx = lax.axis_size("sy"), lax.axis_size("sx")
    sx, sy, rep = (lax.axis_index(a) for a in ("sx", "sy", "rep"))
    odd_x = (sx % 2).astype(jnp.int32)
    odd_y = (sy % 2).astype(jnp.int32)
    cin, planes, rows, width = source.shape
    nf, rows2, width2 = cotan.shape
    c1 = first_kernel.shape[0]
    c2 = nf * n_sy
    own2 = rows // 2
    pairs = 14
    scale = 1.0 / math.sqrt(
        lax.axis_size("rep") * n_sx * n_sy * (planes // 2) * own2 * (width // 2)
    )
    me = sy.astype(jnp.int32).reshape(1)
    odd = odd_x.reshape(1)

    w1 = first_kernel.transpose(2, 3, 4, 1, 0)
    w1q = jnp.concatenate(
        [
            jnp.pad(w1, ((0, 0), (0, 0), (0, 1), (0, 0), (0, 0))),
            jnp.pad(w1, ((0, 0), (0, 0), (1, 0), (0, 0), (0, 0))),
        ],
        axis=-1,
    )
    bias4 = jnp.tile(first_bias, 4)[:, None]
    w2 = second_kernel.transpose(2, 3, 4, 0, 1).reshape(27, nf, c1)
    w2p = jnp.concatenate([w2[:pairs], jnp.pad(w2[pairs:], ((0, 1), (0, 0), (0, 0)))], axis=-1)

    vt, cp = call(
        prep_body,
        "prep",
        [
            jax.ShapeDtypeStruct((planes, rows, cin, width), BF),
            jax.ShapeDtypeStruct((n_sy, own2 + 2, nf, width2), BF),
        ],
        [pltpu.VMEM((rows2 + 2, nf, width2), BF)],
        (me, source, cotan),
        smem_ins=1,
        flops=1 << 30,
    )

    edge_lo, edge_hi = vt[:, 0], vt[:, rows - 1]
    ya = swap_first(jnp.where(odd_y == 1, edge_lo, edge_hi), "sy")
    yb = swap_second(jnp.where(odd_y == 1, edge_hi, edge_lo), "sy")
    rim_lo = jnp.where(odd_y == 1, ya, yb)
    rim_hi = jnp.where(odd_y == 1, yb, ya)
    vr = jnp.concatenate([rim_lo[:, None], vt, rim_hi[:, None]], axis=1)
    za = swap_first(jnp.where(odd_x == 1, vr[0], vr[planes - 1]), "sx")
    zb = swap_second(jnp.where(odd_x == 1, vr[planes - 1], vr[0]), "sx")

    cgot = [cp[0]] + [to_partner(cp[s], "sy", s) for s in range(1, n_sy)]
    co = jnp.stack(cgot)
    ca = swap_first(co, "sx")
    cb = swap_second(co, "sx")
    w2r = jnp.stack([w2p] + [to_partner(w2p, "sy", s) for s in range(1, n_sy)])

    cells, mask, pooled = call(
        conv1_body,
        "conv1",
        [
            jax.ShapeDtypeStruct((planes + 2, rows + 2, 4 * cin, width // 2), BF),
            jax.ShapeDtypeStruct((2, own2 // 2, 4 * c1, width), BF),
            jax.ShapeDtypeStruct((own2, c1, width // 2), BF),
        ],
        [pltpu.VMEM((3, 4 * c1, 16 * cin), BF)],
        (odd, vr, za, zb, w1q, bias4),
        smem_ins=1,
        flops=3 << 30,
    )

    pa = swap_first(jnp.where(odd_y == 1, pooled[0], pooled[own2 - 1]), "sy")
    pb = swap_second(jnp.where(odd_y == 1, pooled[own2 - 1], pooled[0]), "sy")
    ur = jnp.concatenate(
        [
            jnp.where(odd_y == 1, pa, pb)[None],
            pooled,
            jnp.where(odd_y == 1, pb, pa)[None],
        ],
        axis=0,
    )
    ua = swap_first(ur, "sx")
    ub = swap_second(ur, "sx")

    red = call(
        back_body,
        "backward",
        jax.ShapeDtypeStruct((pairs, c2 + cin, 2 * c1), F32),
        [
            pltpu.VMEM((3, own2 + 2, 3, c2, width2), BF),
            pltpu.VMEM((3, c1, 9 * c2), BF),
            pltpu.VMEM((2, own2 // 2, 4 * c1, width), BF),
            pltpu.VMEM((27, c2, 2 * c1), F32),
        ],
        (odd, cells, mask, pooled, co, ca, cb, w2r),
        smem_ins=1,
        flops=6 << 30,
    )

    pieces = call(
        conv2_body,
        "conv2",
        jax.ShapeDtypeStruct((n_sy, own2, nf, width2), BF),
        [pltpu.VMEM((3, own2 + 2, 3, c1, width2), BF)],
        (odd, ur, ua, ub, w2r),
        smem_ins=1,
        flops=1 << 30,
    )
    out_got = [pieces[0]] + [to_partner(pieces[s], "sy", s) for s in range(1, n_sy)]
    bias_wide = jnp.broadcast_to(second_bias[:, None, None], (nf, 1, width2))
    second_out = call(
        unpack_body,
        "unpack",
        jax.ShapeDtypeStruct((nf, rows2, width2), F32),
        [],
        (me, *out_got, bias_wide),
        smem_ins=1,
        flops=1 << 28,
    )

    hp = pairs // 2
    keep = lax.dynamic_slice_in_dim(red, rep * hp, hp, axis=0)
    send = lax.dynamic_slice_in_dim(red, (1 - rep) * hp, hp, axis=0)
    half = keep + swap_first(send, "rep")
    half_bf = half.astype(BF)
    w1_part = half_bf[:, c2:]
    got = [
        to_partner(
            jnp.concatenate([half_bf[:, s * nf : (s + 1) * nf], w1_part], axis=1), "sy", s
        )
        for s in range(1, n_sy)
    ]
    sum2 = tree_sum([half[:, :nf]] + [g[:, :nf].astype(F32) for g in got])
    sum1 = tree_sum([w1_part.astype(F32)] + [g[:, nf:].astype(F32) for g in got])
    both = jnp.concatenate([sum2, sum1], axis=1).astype(BF)
    total = tree_sum(
        [both.astype(F32)] + [to_partner(both, "sx", s).astype(F32) for s in range(1, n_sx)]
    )
    total = total * scale
    other = swap_first(total, "rep")
    full = jnp.where(rep == 0, jnp.stack([total, other]), jnp.stack([other, total]))
    full = full.reshape(pairs, nf + cin, 2 * c1)

    def taps(block):
        wide = jnp.concatenate([block[:, :, :c1], block[:, :, c1:]], axis=0)
        return wide[:27].reshape(3, 3, 3, block.shape[1], c1), wide[27]

    g2, t2 = taps(full[:, :nf])
    g1, t1 = taps(full[:, nf:])
    return (
        second_out[None, :, None],
        g1.transpose(4, 3, 0, 1, 2),
        t1[0],
        g2.transpose(3, 4, 0, 1, 2),
        t2[:, 0],
    )


def solution(mesh):
    placed = (
        P("rep", None, "sx", "sy", None),
        P(),
        P(),
        P("sy", None, None, None, None),
        P("sy"),
        P("rep", "sy", "sx", None, None),
    )
    return jax.shard_map(
        per_device,
        mesh=mesh,
        in_specs=placed,
        out_specs=(
            P("rep", "sy", "sx", None, None),
            P(),
            P(),
            P("sy", None, None, None, None),
            P("sy"),
        ),
        check_vma=False,
    )
```

```python
import functools
import math

import jax
import jax.numpy as jnp
from jax import lax
from jax.experimental import pallas as pl
from jax.experimental.pallas import tpu as pltpu
from jax.sharding import PartitionSpec as P

BF = jnp.bfloat16
F32 = jnp.float32
VMEM_BYTES = 20 * 1024 * 1024


def dot(a, b):
    return jnp.dot(a, b, preferred_element_type=F32)


def dot_nt(a, b):
    return lax.dot_general(a, b, (((1,), (1,)), ((), ())), preferred_element_type=F32)


def index_pair(rows, cols):
    shape = (rows, cols)
    return (
        lax.broadcasted_iota(jnp.int32, shape, 0),
        lax.broadcasted_iota(jnp.int32, shape, 1),
    )


def one_where(cond):
    return jnp.where(cond, 1.0, 0.0).astype(BF)


def swap_majors(outer, inner):
    r, c = index_pair(outer * inner, outer * inner)
    return one_where(lax.rem(r, outer) * inner + lax.div(r, outer) == c)


def shift_both(width):
    r, c = index_pair(width, 2 * width)
    return one_where(((c < width) & (r == c - 1)) | ((c >= width) & (r == c - width + 1)))


def identity(size):
    r, c = index_pair(size, size)
    return one_where(r == c)


def beside(place, below, first, second):
    second = jnp.where(place[5] == 1, second, jnp.zeros_like(second))
    return jnp.where((place[0] == 1) == below, first, second)


def call(body, name, outs, scratch, ins, smem_ins=0, flops=0):
    vm = pl.BlockSpec(memory_space=pltpu.VMEM)
    sm = pl.BlockSpec(memory_space=pltpu.SMEM)
    return pl.pallas_call(
        body,
        name=name,
        out_shape=outs,
        in_specs=[sm] * smem_ins + [vm] * (len(ins) - smem_ins),
        out_specs=jax.tree.map(lambda _: vm, outs),
        scratch_shapes=scratch,
        compiler_params=pltpu.CompilerParams(vmem_limit_bytes=VMEM_BYTES),
        cost_estimate=pl.CostEstimate(flops=flops, bytes_accessed=1 << 20, transcendentals=0),
    )(*ins)


def prep_body(me, vol, cot, w2, vt, cp, w2p, cpad):
    cin, planes, rows, width = vol.shape
    swap = swap_majors(cin, rows)
    half = width // 2
    r, c = index_pair(width, width)
    split = one_where(r == 2 * lax.rem(c, half) + lax.div(c, half))
    for x in range(planes):
        cells = dot(swap, vol[:, x].reshape(cin * rows, width)).astype(BF)
        vt[x] = dot(cells, split).astype(BF).reshape(rows, cin, width)
    nf, rows2, width2 = cot.shape
    step = 16
    swap2 = swap if nf == cin and rows == step else swap_majors(nf, step)
    for h in range(0, rows2, step):
        got = dot(swap2, cot[:, h : h + step].reshape(nf * step, width2))
        cpad[1 + h : 1 + h + step] = got.astype(BF).reshape(step, nf, width2)
    zero = jnp.zeros((1, nf, width2), BF)
    cpad[0:1] = zero
    cpad[rows2 + 1 : rows2 + 2] = zero
    count, rim_rows = cp.shape[0], cp.shape[1]
    for s in range(count):
        cp[s] = cpad[pl.ds((me[0] ^ s) * (rim_rows - 2), rim_rows)]
    taps, _, c1 = w2.shape
    pairs = w2p.shape[0]
    r, c = index_pair(c1, 2 * c1)
    low = dot(w2[:pairs].reshape(pairs * nf, c1), one_where(r == c))
    high = dot(w2[pairs:].reshape((taps - pairs) * nf, c1), one_where(r + c1 == c))
    for p in range(pairs):
        both = low[p * nf : (p + 1) * nf]
        if p + pairs < taps:
            both = both + high[p * nf : (p + 1) * nf]
        w2p[p] = both.astype(BF)


def conv1_body(place, vr, za, zb, w1q, bias, cells, mask, pooled, w1b):
    planes, rows, cin, width = vr.shape
    half = width // 2
    c1 = bias.shape[0] // 4
    eye = identity(4 * c1)
    nothing = jnp.zeros((cin, 2 * c1), BF)
    for i in range(3):
        blocks = []
        for ys in range(4):
            for slot in range(4):
                left = w1q[i, ys, slot] if ys < 3 else nothing
                right = w1q[i, ys - 1, slot] if ys > 0 else nothing
                blocks.append(jnp.concatenate([left, right], axis=1))
        w1b[i] = dot_nt(eye, jnp.concatenate(blocks, axis=0)).astype(BF)
    r, c = index_pair(width, width)
    moved = one_where(
        ((c < half) & (c > 0) & (r == half + c - 1)) | ((c >= half) & (r == c - half + 1) & (r < half))
    )
    for x in range(planes + 2):
        if x in (0, planes + 1):
            plane = beside(place, x == 0, za[...], zb[...])
        else:
            plane = vr[x - 1]
        out = dot(plane.reshape(rows * cin, width), moved).astype(BF).reshape(rows, cin, width)
        cells[x, :, 0:cin] = out[:, :, :half]
        cells[x, :, cin : 2 * cin] = plane[:, :, :half]
        cells[x, :, 2 * cin : 3 * cin] = plane[:, :, half:]
        cells[x, :, 3 * cin : 4 * cin] = out[:, :, half:]
    rows2 = pooled.shape[0]
    deep = 16 * cin
    for t in range(rows2 // 2):
        total = None
        for xp in range(2):
            acc = None
            for i in range(3):
                rhs = jnp.concatenate(
                    [
                        cells[xp + i, 4 * t : 4 * t + 4].reshape(deep, half),
                        cells[xp + i, 4 * t + 2 : 4 * t + 6].reshape(deep, half),
                    ],
                    axis=1,
                )
                part = dot(w1b[i], rhs)
                acc = part if acc is None else acc + part
            pre = acc + bias[...]
            above = pre > 0
            flags = jnp.where(above, 1.0, 0.0).astype(BF)
            if t > 0:
                mask[xp, 2 * t - 1] = flags[:, :half]
            if 2 * t < rows2 - 2:
                mask[xp, 2 * t] = flags[:, half:]
            act = jnp.where(above, pre, 0.3 * pre)
            for b in range(4):
                piece = act[b * c1 : (b + 1) * c1]
                total = piece if total is None else total + piece
        mean = (total * 0.125).astype(BF)
        first, second = mean[:, :half], mean[:, half:]
        if t == 0:
            first = jnp.where(place[1] == 1, first, jnp.zeros_like(first))
        if t == rows2 // 2 - 1:
            second = jnp.where(place[2] == 1, second, jnp.zeros_like(second))
        pooled[2 * t] = first
        pooled[2 * t + 1] = second


def with_shifts(store, plane, shifts):
    rows, chans, width = plane.shape
    out = dot(plane.reshape(rows * chans, width), shifts).astype(BF).reshape(rows, chans, 2 * width)
    store(0, out[:, :, :width])
    store(1, plane)
    store(2, out[:, :, width:])


def conv2_body(place, ur, ua, ub, w2r, pieces, u):
    rows, c1, width = ur.shape
    count, pairs, nf, _ = w2r.shape
    shifts = shift_both(width)
    planes = (
        beside(place, True, ua[...], ub[...]),
        ur[...],
        beside(place, False, ua[...], ub[...]),
    )
    for x in range(3):

        def store(k, value, x=x):
            u[x, :, k] = value

        with_shifts(store, planes[x], shifts)
    weights = jnp.concatenate(
        [jnp.concatenate([w2r[s, p] for s in range(count)], axis=0) for p in range(pairs)], axis=1
    )

    def tap(y, d):
        d = d if d < 27 else 0
        return u[d // 9, y + (d // 3) % 3, d % 3]

    def deep(y):
        return jnp.concatenate(
            [tap(y, d) for p in range(pairs) for d in (p, p + pairs)], axis=0
        )

    for y in range(0, rows - 2, 2):
        rhs = jnp.concatenate([deep(y), deep(y + 1)], axis=1)
        out = dot(weights, rhs).astype(BF)
        for s in range(count):
            pieces[s, y] = out[s * nf : (s + 1) * nf, :width]
            pieces[s, y + 1] = out[s * nf : (s + 1) * nf, width:]


def own_body(co, pooled, w2r, wb, own_back, own_g2, own_b2, t_ref):
    count, rows, nf, width = co.shape
    pairs = w2r.shape[1]
    c1 = pooled.shape[1]
    c2 = count * nf
    fill_planes(t_ref, co, shift_both(width))
    eye = identity(2 * c1)
    for p in range(pairs):
        block = jnp.concatenate([w2r[s, p] for s in range(count)], axis=0)
        turned = dot_nt(eye, block)
        for half, d in ((0, p), (1, p + pairs)):
            if d < 27:
                i, j, k = d // 9, (d // 3) % 3, d % 3
                at = ((2 - j) * 3 + (2 - k)) * c2
                wb[2 - i, :, at : at + c2] = turned[half * c1 : (half + 1) * c1].astype(BF)
    for t in range((rows - 2) // 2):
        own_back[t] = dot(wb[1], pair_rows(t_ref, t))
    rhs = pooled_wide(pooled)
    for ys in range(3):
        out = dot_nt(rows_wide(t_ref, ys, rows - 2), rhs)
        for zs in range(3):
            own_g2[(2 - ys) * 3 + (2 - zs)] = out[zs * c2 : (zs + 1) * c2]
    sums = None
    for y in range(1, rows - 1):
        v = t_ref[y, 1].astype(F32)
        sums = v if sums is None else sums + v
    own_b2[...] = jnp.broadcast_to(jnp.sum(sums, axis=1, keepdims=True), own_b2.shape)


def fill_planes(t_ref, plane, shifts):
    nf = plane.shape[2]
    for s in range(plane.shape[0]):

        def store(k, value, s=s):
            t_ref[:, k, s * nf : (s + 1) * nf] = value

        with_shifts(store, plane[s], shifts)


def pair_rows(t_ref, t):
    rows, slots, chans, width = t_ref.shape
    return jnp.concatenate(
        [t_ref[2 * t + n : 2 * t + n + 3].reshape(3 * slots * chans, width) for n in range(2)],
        axis=1,
    )


def rows_wide(t_ref, ys, count):
    rows, slots, chans, width = t_ref.shape
    return jnp.concatenate(
        [t_ref[y + ys].reshape(slots * chans, width) for y in range(count)], axis=1
    )


def pooled_wide(pooled):
    return jnp.concatenate(
        [
            jnp.concatenate([pooled[y], pooled[y]], axis=0)
            for y in range(1, pooled.shape[0] - 1)
        ],
        axis=1,
    )


def back_body(place, cells, mask, pooled, ca, cb, wb, own_back, own_g2, own_b2,
              keep, send, t0, t2, gp, g2, red):
    count, rows, nf, width = ca.shape
    pairs = 14
    c1 = pooled.shape[1]
    c2 = count * nf
    cin = cells.shape[2] // 4
    shifts = shift_both(width)
    fill_planes(t0, beside(place, True, ca[...], cb[...]), shifts)
    fill_planes(t2, beside(place, False, ca[...], cb[...]), shifts)
    bias1 = jnp.zeros((8, 4 * c1), F32)
    ones = jnp.ones((8, 2 * width), BF)
    n_pairs = (rows - 2) // 2
    for t in range(n_pairs):
        acc = own_back[t] + dot(wb[0], pair_rows(t0, t)) + dot(wb[2], pair_rows(t2, t))
        eighth = acc * 0.125
        spread = jnp.concatenate([eighth] * 4, axis=0)
        for xp in range(2):
            flags = jnp.concatenate([mask[xp, 2 * t], mask[xp, 2 * t + 1]], axis=1)
            grad = (spread * jnp.where(flags > 0, 1.0, 0.3)).astype(BF)
            gp[xp, t] = grad
            bias1 = bias1 + dot_nt(ones, grad)
    rhs = pooled_wide(pooled)
    for x, t_ref in ((0, t0), (2, t2)):
        for ys in range(3):
            out = dot_nt(rows_wide(t_ref, ys, rows - 2), rhs)
            for zs in range(3):
                d = ((2 - x) * 3 + (2 - ys)) * 3 + (2 - zs)
                g2[d] = out[zs * c2 : (zs + 1) * c2]

    def part2(d):
        if d == 27:
            return own_b2[...]
        return own_g2[d - 9] if 9 <= d < 18 else g2[d]

    parts = keep.shape[0]
    hp = pairs // 2
    share2, share1 = nf // parts, cin // parts
    low_wide = lax.broadcasted_iota(jnp.int32, (c2, 2 * c1), 1) < c1

    def put(p, start, share, block):
        for part in range(parts):
            red[p // hp, part, p % hp, start : start + share] = block[
                part * share : (part + 1) * share
            ]

    for p in range(pairs):
        wide = jnp.where(low_wide, part2(p), part2(p + pairs))
        for s in range(count):
            put(p, s * share2, share2, wide[s * nf : (s + 1) * nf])
    lane = lax.broadcasted_iota(jnp.int32, (cin, 2 * c1), 1)
    low_half = lane < c1
    lows, highs = {}, {}
    for i in range(3):
        acc = None
        for xp in range(2):
            for t in range(n_pairs):
                lhs = jnp.concatenate(
                    [
                        cells[xp + i, 4 * t + 2 : 4 * t + 6].reshape(16 * cin, width),
                        cells[xp + i, 4 * t + 4 : 4 * t + 8].reshape(16 * cin, width),
                    ],
                    axis=1,
                )
                part = dot_nt(lhs, gp[xp, t])
                acc = part if acc is None else acc + part
        for j in range(3):
            slots = []
            for slot in range(4):
                r0 = (j * 4 + slot) * cin
                r1 = ((j + 1) * 4 + slot) * cin
                slots.append(acc[r0 : r0 + cin, : 2 * c1] + acc[r1 : r1 + cin, 2 * c1 :])
            turned = [pltpu.roll(v, c1, 1) for v in slots]
            for k in range(3):
                d = (i * 3 + j) * 3 + k
                if d < pairs:
                    lows[d] = slots[k] + turned[k + 1]
                else:
                    highs[d - pairs] = slots[k + 1] + turned[k]
    b1 = bias1[:, : 2 * c1] + bias1[:, 2 * c1 :]
    b1 = b1 + pltpu.roll(b1, c1, 1)
    highs[pairs - 1] = jnp.concatenate([b1] * (cin // 8), axis=0)
    for p in range(pairs):
        put(p, count * share2, share1, jnp.where(low_half, lows[p], highs[p]))
    for part in range(parts):
        keep[part] = red[place[4], part ^ place[3]]
        send[part] = red[1 - place[4], part ^ place[3]]


def unpack_body(me, *refs):
    pieces, bias, out = refs[:-2], refs[-2], refs[-1]
    nf, _, width = bias.shape
    rows = out.shape[1] // len(pieces)
    swap = swap_majors(rows, nf)
    for s, piece in enumerate(pieces):
        got = dot(swap, piece[: rows * nf]).reshape(nf, rows, width)
        out[:, pl.ds(pl.multiple_of((me[0] ^ s) * rows, rows), rows), :] = got + bias[...]


def finish_body(place, mine, other, g2, b2, g1, b1):
    parts, hp, _, width = mine.shape
    nf, cin, c1 = g2.shape[1], g1.shape[1], g2.shape[2]
    share2, share1 = nf // parts, cin // parts
    first = place[4] == 0
    for part in range(parts):
        slot = part ^ place[3]
        got = mine[slot].astype(F32)
        more = other[slot].astype(F32)
        halves = (jnp.where(first, got, more), jnp.where(first, more, got))
        for p in range(2 * hp):
            block = halves[p // hp][p % hp]
            turned = pltpu.roll(block, c1, 1)
            for d, v in ((p, block), (p + 2 * hp, turned)):
                low = v[:share2, :c1]
                high = v[share2:, :c1]
                if d < 27:
                    g2[d, part * share2 : (part + 1) * share2] = low
                    g1[d, part * share1 : (part + 1) * share1] = high
                else:
                    b2[part * share2 : (part + 1) * share2] = low
                    if part == 0:
                        b1[0:1] = high[0:1]


def swap_first(value, axis):
    count = lax.axis_size(axis)
    return lax.ppermute(value, axis, [(i, i ^ 1) for i in range(count)])


def swap_second(value, axis):
    count = lax.axis_size(axis)
    both = lax.axis_size("rep")
    pairs = []
    for i in range(count):
        for r in range(both):
            if i in (0, count - 1):
                pairs.append((i * both + r, i * both + (r ^ 1)))
            else:
                pairs.append((i * both + r, (i + 1 if i % 2 else i - 1) * both + r))
    return lax.ppermute(value, (axis, "rep"), pairs)


def to_partner(value, axis, s):
    count = lax.axis_size(axis)
    return lax.ppermute(value, axis, [(i, i ^ s) for i in range(count)])


def tree_sum(values):
    values = list(values)
    while len(values) > 1:
        values = [values[n] + values[n + 1] for n in range(0, len(values), 2)]
    return values[0]


def per_device(volume, first_kernel, first_bias, second_kernel, second_bias, cotangent):
    source = volume[0]
    cotan = cotangent[0, :, 0]
    n_sy, n_sx = lax.axis_size("sy"), lax.axis_size("sx")
    sx, sy, rep = (lax.axis_index(a) for a in ("sx", "sy", "rep"))
    odd_x = (sx % 2).astype(jnp.int32)
    odd_y = (sy % 2).astype(jnp.int32)
    cin, planes, rows, width = source.shape
    nf, rows2, width2 = cotan.shape
    c1 = first_kernel.shape[0]
    c2 = nf * n_sy
    own2 = rows // 2
    pairs = 14
    scale = 1.0 / math.sqrt(
        lax.axis_size("rep") * n_sx * n_sy * (planes // 2) * own2 * (width // 2)
    )
    me = sy.astype(jnp.int32).reshape(1)
    place = jnp.stack(
        [
            jnp.asarray(v, jnp.int32)
            for v in (odd_x, sy > 0, sy < n_sy - 1, sx, rep, (sx > 0) & (sx < n_sx - 1))
        ]
    )
    rim = 3

    w1 = first_kernel.transpose(2, 3, 4, 1, 0)
    w1q = jnp.concatenate(
        [
            jnp.pad(w1, ((0, 0), (0, 0), (0, 1), (0, 0), (0, 0))),
            jnp.pad(w1, ((0, 0), (0, 0), (1, 0), (0, 0), (0, 0))),
        ],
        axis=-1,
    )
    bias4 = jnp.tile(first_bias, 4)[:, None]
    w2 = second_kernel.transpose(2, 3, 4, 0, 1).reshape(27, nf, c1)
    vt, cp, w2p = call(
        prep_body,
        "prep",
        [
            jax.ShapeDtypeStruct((planes, rows, cin, width), BF),
            jax.ShapeDtypeStruct((n_sy, own2 + 2, nf, width2), BF),
            jax.ShapeDtypeStruct((pairs, nf, 2 * c1), BF),
        ],
        [pltpu.VMEM((rows2 + 2, nf, width2), BF)],
        (me, source, cotan, w2),
        smem_ins=1,
        flops=1 << 30,
    )

    edge_lo, edge_hi = vt[:, :rim], vt[:, rows - rim :]
    ya = swap_first(jnp.where(odd_y == 1, edge_lo, edge_hi), "sy")
    yb = swap_second(jnp.where(odd_y == 1, edge_hi, edge_lo), "sy")
    yb = jnp.where((sy > 0) & (sy < n_sy - 1), yb, jnp.zeros_like(yb))
    rim_lo = jnp.where(odd_y == 1, ya, yb)
    rim_hi = jnp.where(odd_y == 1, yb, ya)
    vr = jnp.concatenate([rim_lo, vt, rim_hi], axis=1)
    za = swap_first(jnp.where(odd_x == 1, vr[0], vr[planes - 1]), "sx")
    zb = swap_second(jnp.where(odd_x == 1, vr[planes - 1], vr[0]), "sx")

    co = jnp.stack([cp[0]] + [to_partner(cp[s], "sy", s) for s in range(1, n_sy)])
    ca = swap_first(co, "sx")
    cb = swap_second(co, "sx")
    w2p, vr = lax.optimization_barrier((w2p, vr))
    w2r = jnp.stack([w2p] + [to_partner(w2p, "sy", s) for s in range(1, n_sy)])

    cells, mask, pooled = call(
        conv1_body,
        "conv1",
        [
            jax.ShapeDtypeStruct((planes + 2, rows + 2 * rim, 4 * cin, width // 2), BF),
            jax.ShapeDtypeStruct((2, own2, 4 * c1, width // 2), BF),
            jax.ShapeDtypeStruct((own2 + 2, c1, width // 2), BF),
        ],
        [pltpu.VMEM((3, 4 * c1, 16 * cin), BF)],
        (place, vr, za, zb, w1q, bias4),
        smem_ins=1,
        flops=3 << 30,
    )
    ua = swap_first(pooled, "sx")
    ub = swap_second(pooled, "sx")

    ca, cb, ua, ub = lax.optimization_barrier((ca, cb, ua, ub))

    plane_shape = (own2 + 2, 3, c2, width2)
    wb, own_back, own_g2, own_b2 = call(
        own_body,
        "backward_own",
        [
            jax.ShapeDtypeStruct((3, c1, 9 * c2), BF),
            jax.ShapeDtypeStruct((own2 // 2, c1, 2 * width2), F32),
            jax.ShapeDtypeStruct((9, c2, 2 * c1), F32),
            jax.ShapeDtypeStruct((c2, 2 * c1), F32),
        ],
        [pltpu.VMEM(plane_shape, BF)],
        (co, pooled, w2r),
        flops=2 << 30,
    )
    hp = pairs // 2
    share = (c2 + cin) // n_sx
    half_shape = jax.ShapeDtypeStruct((n_sx, hp, share, 2 * c1), F32)
    keep, send = call(
        back_body,
        "backward",
        [half_shape, half_shape],
        [
            pltpu.VMEM(plane_shape, BF),
            pltpu.VMEM(plane_shape, BF),
            pltpu.VMEM((2, own2 // 2, 4 * c1, width), BF),
            pltpu.VMEM((27, c2, 2 * c1), F32),
            pltpu.VMEM((2, *half_shape.shape), F32),
        ],
        (place, cells, mask, pooled, ca, cb, wb, own_back, own_g2, own_b2),
        smem_ins=1,
        flops=5 << 30,
    )

    half = keep + swap_first(send, "rep")
    half, ua, ub = lax.optimization_barrier((half, ua, ub))
    pieces = call(
        conv2_body,
        "conv2",
        jax.ShapeDtypeStruct((n_sy, own2, nf, width2), BF),
        [pltpu.VMEM((3, own2 + 2, 3, c1, width2), BF)],
        (place, pooled, ua, ub, w2r),
        smem_ins=1,
        flops=1 << 30,
    )
    part = tree_sum(
        [half[0]]
        + [to_partner(half[s].astype(BF), "sx", s).astype(F32) for s in range(1, n_sx)]
    )
    own_rows = own2 * nf
    share2, share1 = nf // n_sx, cin // n_sx
    part_bf = part.astype(BF)
    tail = part_bf[:, n_sy * share2 :]

    def sy_message(s):
        w2_rows = part_bf[:, s * share2 : (s + 1) * share2]
        return jnp.concatenate(
            [
                pieces[s].reshape(own_rows, width2),
                jnp.concatenate([w2_rows, tail], axis=1).reshape(-1, width2),
            ],
            axis=0,
        )

    own_piece = pieces[0].reshape(own_rows, width2)
    passed = [to_partner(sy_message(s), "sy", s) for s in range(1, n_sy)]
    bias_wide = jnp.broadcast_to(second_bias[:, None, None], (nf, 1, width2))
    second_out = call(
        unpack_body,
        "unpack",
        jax.ShapeDtypeStruct((nf, rows2, width2), F32),
        [],
        (me, own_piece, *passed, bias_wide),
        smem_ins=1,
        flops=1 << 28,
    )
    sums = [g[own_rows:].reshape(hp, share2 + share1, width2).astype(F32) for g in passed]
    own = jnp.concatenate([part[:, :share2], tail.astype(F32)], axis=1)
    total = (tree_sum([own] + sums) * scale).astype(BF)
    spread = jnp.stack([total] + [to_partner(total, "sx", s) for s in range(1, n_sx)])
    spread, second_out = lax.optimization_barrier((spread, second_out))
    other = swap_first(spread, "rep")
    g2, t2, g1, t1 = call(
        finish_body,
        "finish",
        [
            jax.ShapeDtypeStruct((27, nf, c1), F32),
            jax.ShapeDtypeStruct((nf, c1), F32),
            jax.ShapeDtypeStruct((27, cin, c1), F32),
            jax.ShapeDtypeStruct((1, c1), F32),
        ],
        [],
        (place, spread, other),
        smem_ins=1,
        flops=1 << 20,
    )
    return (
        second_out[None, :, None],
        g1.reshape(3, 3, 3, cin, c1).transpose(4, 3, 0, 1, 2),
        t1[0],
        g2.reshape(3, 3, 3, nf, c1).transpose(3, 4, 0, 1, 2),
        t2[:, 0],
    )


def solution(mesh):
    placed = (
        P("rep", None, "sx", "sy", None),
        P(),
        P(),
        P("sy", None, None, None, None),
        P("sy"),
        P("rep", "sy", "sx", None, None),
    )
    return jax.shard_map(
        per_device,
        mesh=mesh,
        in_specs=placed,
        out_specs=(
            P("rep", "sy", "sx", None, None),
            P(),
            P(),
            P("sy", None, None, None, None),
            P("sy"),
        ),
        check_vma=False,
    )
```

```python
import math

import jax
import jax.numpy as jnp
from jax import lax
from jax.experimental import pallas as pl
from jax.experimental.pallas import tpu as pltpu
from jax.sharding import PartitionSpec as P

BF = jnp.bfloat16
F32 = jnp.float32


def dot(a, b):
    return jnp.dot(a, b, preferred_element_type=F32)


def dot_nt(a, b):
    return lax.dot_general(a, b, (((1,), (1,)), ((), ())), preferred_element_type=F32)


def index_pair(rows, cols):
    shape = (rows, cols)
    return (
        lax.broadcasted_iota(jnp.int32, shape, 0),
        lax.broadcasted_iota(jnp.int32, shape, 1),
    )


def one_where(cond):
    return jnp.where(cond, 1.0, 0.0).astype(BF)


def swap_majors(outer, inner):
    r, c = index_pair(outer * inner, outer * inner)
    return one_where(lax.rem(r, outer) * inner + lax.div(r, outer) == c)


def shift_both(width):
    r, c = index_pair(width, 2 * width)
    return one_where(((c < width) & (r == c - 1)) | ((c >= width) & (r == c - width + 1)))


def identity(size):
    r, c = index_pair(size, size)
    return one_where(r == c)


def beside(place, below, first, second):
    use_first = jnp.where((place[0] == 1) == below, 1.0, 0.0)
    use_second = (1.0 - use_first) * jnp.where(place[5] == 1, 1.0, 0.0)
    lanes = (1, first.shape[-1])
    return first[...] * jnp.full(lanes, use_first, F32).astype(BF) + second[...] * jnp.full(
        lanes, use_second, F32
    ).astype(BF)


def call(body, name, outs, scratch, ins, smem_ins=0, flops=0, room=40):
    vm = pl.BlockSpec(memory_space=pltpu.VMEM)
    sm = pl.BlockSpec(memory_space=pltpu.SMEM)
    return pl.pallas_call(
        body,
        name=name,
        out_shape=outs,
        in_specs=[sm] * smem_ins + [vm] * (len(ins) - smem_ins),
        out_specs=jax.tree.map(lambda _: vm, outs),
        scratch_shapes=scratch,
        compiler_params=pltpu.CompilerParams(vmem_limit_bytes=room << 20),
        cost_estimate=pl.CostEstimate(flops=flops, bytes_accessed=1 << 20, transcendentals=0),
    )(*ins)


def volume_body(vol, vt):
    planes, rows, cin, width = vt.shape
    swap = swap_majors(cin, rows)
    half = width // 2
    r, c = index_pair(width, width)
    split = one_where(r == 2 * lax.rem(c, half) + lax.div(c, half))
    for x in range(planes):
        cells = dot(swap, vol[:, x].reshape(cin * rows, width)).astype(BF)
        vt[x] = dot(cells, split).astype(BF).reshape(rows, cin, width)


def prep_body(me, cot, w2, cp, w2p, cpad):
    nf, rows2, width2 = cot.shape
    step = 16
    swap2 = swap_majors(nf, step)
    for h in range(0, rows2, step):
        got = dot(swap2, cot[:, h : h + step].reshape(nf * step, width2))
        cpad[1 + h : 1 + h + step] = got.astype(BF).reshape(step, nf, width2)
    zero = jnp.zeros((1, nf, width2), BF)
    cpad[0:1] = zero
    cpad[rows2 + 1 : rows2 + 2] = zero
    count, rim_rows = cp.shape[0], cp.shape[1]
    for s in range(count):
        cp[s] = cpad[pl.ds((me[0] ^ s) * (rim_rows - 2), rim_rows)]
    taps, _, c1 = w2.shape
    pairs = w2p.shape[0]
    r, c = index_pair(c1, 2 * c1)
    low = dot(w2[:pairs].reshape(pairs * nf, c1), one_where(r == c))
    high = dot(w2[pairs:].reshape((taps - pairs) * nf, c1), one_where(r + c1 == c))
    for p in range(pairs):
        both = low[p * nf : (p + 1) * nf]
        if p + pairs < taps:
            both = both + high[p * nf : (p + 1) * nf]
        w2p[p] = both.astype(BF)


def moved_by_one(width):
    half = width // 2
    r, c = index_pair(width, width)
    return one_where(
        ((c < half) & (c > 0) & (r == half + c - 1))
        | ((c >= half) & (r == c - half + 1) & (r < half))
    )


def fill_cells(cells, plane, moved):
    rows, cin, width = plane.shape
    half = width // 2
    out = dot(plane.reshape(rows * cin, width), moved).astype(BF).reshape(rows, cin, width)
    cells[:, 0:cin] = out[:, :, :half]
    cells[:, cin : 2 * cin] = plane[:, :, :half]
    cells[:, 2 * cin : 3 * cin] = plane[:, :, half:]
    cells[:, 3 * cin : 4 * cin] = out[:, :, half:]


def two_rows(cells, first):
    rows, deep, half = cells.shape
    return jnp.concatenate(
        [cells[first + 2 * n : first + 2 * n + 4].reshape(4 * deep, half) for n in range(2)],
        axis=1,
    )


def conv1_own_body(vr, w1q, bias, cells, w1b, acc):
    planes, rows, cin, width = vr.shape
    c1 = bias.shape[0] // 4
    eye = identity(4 * c1)
    nothing = jnp.zeros((cin, 2 * c1), BF)
    for i in range(3):
        blocks = []
        for ys in range(4):
            for slot in range(4):
                left = w1q[i, ys, slot] if ys < 3 else nothing
                right = w1q[i, ys - 1, slot] if ys > 0 else nothing
                blocks.append(jnp.concatenate([left, right], axis=1))
        w1b[i] = dot_nt(eye, jnp.concatenate(blocks, axis=0)).astype(BF)
    moved = moved_by_one(width)
    for x in range(planes):
        fill_cells(cells.at[x], vr[x], moved)
    for t in range(acc.shape[1]):
        for xp in range(2):
            acc[xp, t] = (
                dot(w1b[1 - xp], two_rows(cells.at[0], 4 * t))
                + dot(w1b[2 - xp], two_rows(cells.at[1], 4 * t))
                + bias[...]
            )


def conv1_body(place, za, zb, w1b, acc, low, high, mask, pooled):
    rows, cin, width = za.shape
    half = width // 2
    c1 = pooled.shape[1]
    moved = moved_by_one(width)
    fill_cells(low, beside(place, True, za, zb), moved)
    fill_cells(high, beside(place, False, za, zb), moved)
    rows2 = pooled.shape[0]
    for t in range(rows2 // 2):
        total = None
        for xp, cells in ((0, low), (1, high)):
            pre = acc[xp, t] + dot(w1b[2 * xp], two_rows(cells, 4 * t))
            above = pre > 0
            flags = jnp.where(above, 1.0, 0.0).astype(BF)
            if t > 0:
                mask[xp, 2 * t - 1] = flags[:, :half]
            if 2 * t < rows2 - 2:
                mask[xp, 2 * t] = flags[:, half:]
            act = jnp.where(above, pre, 0.3 * pre)
            for b in range(4):
                piece = act[b * c1 : (b + 1) * c1]
                total = piece if total is None else total + piece
        if t == 0:
            total = total * jnp.where(at_low(total, half) & (place[1] == 0), 0.0, 1.0)
        if t == rows2 // 2 - 1:
            total = total * jnp.where(at_low(total, half) | (place[2] == 1), 1.0, 0.0)
        mean = (total * 0.125).astype(BF)
        pooled[2 * t] = mean[:, :half]
        pooled[2 * t + 1] = mean[:, half:]


def at_low(value, half):
    return lax.broadcasted_iota(jnp.int32, value.shape, 1) < half


def with_shifts(store, plane, shifts):
    rows, chans, width = plane.shape
    out = dot(plane.reshape(rows * chans, width), shifts).astype(BF).reshape(rows, chans, 2 * width)
    store(0, out[:, :, :width])
    store(1, plane)
    store(2, out[:, :, width:])


def conv2_body(place, ur, ua, ub, w2r, pieces, u):
    rows, c1, width = ur.shape
    count, pairs, nf, _ = w2r.shape
    shifts = shift_both(width)
    planes = (beside(place, True, ua, ub), ur[...], beside(place, False, ua, ub))
    for x in range(3):

        def store(k, value, x=x):
            u[x, :, k] = value

        with_shifts(store, planes[x], shifts)
    weights = jnp.concatenate(
        [jnp.concatenate([w2r[s, p] for s in range(count)], axis=0) for p in range(pairs)], axis=1
    )

    def tap(y, d):
        d = d if d < 27 else 0
        return u[d // 9, y + (d // 3) % 3, d % 3]

    def deep(y):
        return jnp.concatenate(
            [tap(y, d) for p in range(pairs) for d in (p, p + pairs)], axis=0
        )

    for y in range(0, rows - 2, 2):
        rhs = jnp.concatenate([deep(y), deep(y + 1)], axis=1)
        out = dot(weights, rhs).astype(BF)
        for s in range(count):
            pieces[s, y] = out[s * nf : (s + 1) * nf, :width]
            pieces[s, y + 1] = out[s * nf : (s + 1) * nf, width:]


def own_body(co, pooled, w2r, wb, own_back, own_g2, own_b2, t_ref):
    count, rows, nf, width = co.shape
    pairs = w2r.shape[1]
    c1 = pooled.shape[1]
    c2 = count * nf
    fill_planes(t_ref, co, shift_both(width))
    eye = identity(2 * c1)
    for p in range(pairs):
        block = jnp.concatenate([w2r[s, p] for s in range(count)], axis=0)
        turned = dot_nt(eye, block)
        for half, d in ((0, p), (1, p + pairs)):
            if d < 27:
                i, j, k = d // 9, (d // 3) % 3, d % 3
                at = ((2 - j) * 3 + (2 - k)) * c2
                wb[2 - i, :, at : at + c2] = turned[half * c1 : (half + 1) * c1].astype(BF)
    for t in range((rows - 2) // 2):
        own_back[t] = dot(wb[1], pair_rows(t_ref, t))
    rhs = pooled_wide(pooled)
    for ys in range(3):
        out = dot_nt(rows_wide(t_ref, ys, rows - 2), rhs)
        for zs in range(3):
            own_g2[(2 - ys) * 3 + (2 - zs)] = out[zs * c2 : (zs + 1) * c2]
    sums = None
    for y in range(1, rows - 1):
        v = t_ref[y, 1].astype(F32)
        sums = v if sums is None else sums + v
    own_b2[...] = jnp.broadcast_to(jnp.sum(sums, axis=1, keepdims=True), own_b2.shape)


def fill_planes(t_ref, plane, shifts):
    nf = plane.shape[2]
    for s in range(plane.shape[0]):

        def store(k, value, s=s):
            t_ref[:, k, s * nf : (s + 1) * nf] = value

        with_shifts(store, plane[s], shifts)


def pair_rows(t_ref, t):
    rows, slots, chans, width = t_ref.shape
    return jnp.concatenate(
        [t_ref[2 * t + n : 2 * t + n + 3].reshape(3 * slots * chans, width) for n in range(2)],
        axis=1,
    )


def rows_wide(t_ref, ys, count):
    rows, slots, chans, width = t_ref.shape
    return jnp.concatenate(
        [t_ref[y + ys].reshape(slots * chans, width) for y in range(count)], axis=1
    )


def pooled_wide(pooled):
    return jnp.concatenate(
        [
            jnp.concatenate([pooled[y], pooled[y]], axis=0)
            for y in range(1, pooled.shape[0] - 1)
        ],
        axis=1,
    )


def back_body(place, mask, pooled, ca, cb, wb, own_back, gp, g2, bias1, t0, t2):
    count, rows, nf, width = ca.shape
    c1 = pooled.shape[1]
    c2 = count * nf
    shifts = shift_both(width)
    fill_planes(t0, beside(place, True, ca, cb), shifts)
    fill_planes(t2, beside(place, False, ca, cb), shifts)
    sums = jnp.zeros((8, 4 * c1), F32)
    ones = jnp.ones((8, 2 * width), BF)
    n_pairs = (rows - 2) // 2
    for t in range(n_pairs):
        acc = own_back[t] + dot(wb[0], pair_rows(t0, t)) + dot(wb[2], pair_rows(t2, t))
        eighth = acc * 0.125
        spread = jnp.concatenate([eighth] * 4, axis=0)
        for xp in range(2):
            flags = jnp.concatenate([mask[xp, 2 * t], mask[xp, 2 * t + 1]], axis=1)
            grad = (spread * jnp.where(flags > 0, 1.0, 0.3)).astype(BF)
            gp[xp, t] = grad
            sums = sums + dot_nt(ones, grad)
    bias1[...] = sums
    rhs = pooled_wide(pooled)
    for n, t_ref in enumerate((t0, t2)):
        for ys in range(3):
            out = dot_nt(rows_wide(t_ref, ys, rows - 2), rhs)
            for zs in range(3):
                g2[n, (2 - ys) * 3 + (2 - zs)] = out[zs * c2 : (zs + 1) * c2]


def weights_body(place, cells, low, high, gp, g2, bias1, own_g2, own_b2, keep, send, red):
    c2, wide_lanes = own_b2.shape
    c1 = wide_lanes // 2
    cin = cells.shape[2] // 4
    n_pairs = gp.shape[1]
    pairs = 14
    sources = (low, cells.at[0], cells.at[1], high)

    def part2(d):
        if d == 27:
            return own_b2[...]
        return own_g2[d - 9] if 9 <= d < 18 else g2[1 - d // 18, d % 9]

    low_wide = lax.broadcasted_iota(jnp.int32, (c2, 2 * c1), 1) < c1
    for p in range(pairs):
        red[p, :c2] = jnp.where(low_wide, part2(p), part2(p + pairs))
    lane = lax.broadcasted_iota(jnp.int32, (cin, 2 * c1), 1)
    low_half = lane < c1
    lows, highs = {}, {}
    for i in range(3):
        acc = None
        for xp in range(2):
            for t in range(n_pairs):
                lhs = two_rows(sources[xp + i], 4 * t + 2)
                part = dot_nt(lhs, gp[xp, t])
                acc = part if acc is None else acc + part
        for j in range(3):
            slots = []
            for slot in range(4):
                r0 = (j * 4 + slot) * cin
                r1 = ((j + 1) * 4 + slot) * cin
                slots.append(acc[r0 : r0 + cin, : 2 * c1] + acc[r1 : r1 + cin, 2 * c1 :])
            turned = [pltpu.roll(v, c1, 1) for v in slots]
            for k in range(3):
                d = (i * 3 + j) * 3 + k
                if d < pairs:
                    lows[d] = slots[k] + turned[k + 1]
                else:
                    highs[d - pairs] = slots[k + 1] + turned[k]
    b1 = bias1[:, : 2 * c1] + bias1[:, 2 * c1 :]
    b1 = b1 + pltpu.roll(b1, c1, 1)
    highs[pairs - 1] = jnp.concatenate([b1] * (cin // 8), axis=0)
    for p in range(pairs):
        red[p, c2:] = jnp.where(low_half, lows[p], highs[p])
    hp = pairs // 2
    keep[...] = red[pl.ds(place[4] * hp, hp)]
    send[...] = red[pl.ds((1 - place[4]) * hp, hp)]


def unpack_body(me, *refs):
    pieces, bias, out = refs[:-2], refs[-2], refs[-1]
    nf, _, width = bias.shape
    rows = out.shape[1] // len(pieces)
    swap = swap_majors(rows, nf)
    for s, piece in enumerate(pieces):
        got = dot(swap, piece[: rows * nf]).reshape(nf, rows, width)
        out[:, pl.ds(pl.multiple_of((me[0] ^ s) * rows, rows), rows), :] = got + bias[...]


def finish_body(place, mine, other, g2, b2, g1, b1):
    hp, _, width = mine.shape
    nf, c1 = g2.shape[1], g2.shape[2]
    first = place[4] == 0
    got, more = mine[...], other[...]
    halves = (jnp.where(first, got, more), jnp.where(first, more, got))
    for p in range(2 * hp):
        block = halves[p // hp][p % hp]
        turned = pltpu.roll(block, c1, 1)
        for d, v in ((p, block), (p + 2 * hp, turned)):
            low, high = v[:nf, :c1], v[nf:, :c1]
            if d < 27:
                g2[d] = low
                g1[d] = high
            else:
                column = lax.broadcasted_iota(jnp.int32, low.shape, 0)
                lane = lax.broadcasted_iota(jnp.int32, low.shape, 1)
                row = jnp.sum(jnp.where(column == lane, low, 0.0), axis=0, keepdims=True)
                b2[...] = row[:, :nf]
                b1[...] = high[0:1]


def swap_first(value, axis):
    count = lax.axis_size(axis)
    return lax.ppermute(value, axis, [(i, i ^ 1) for i in range(count)])


def swap_second(value, axis):
    count = lax.axis_size(axis)
    both = lax.axis_size("rep")
    pairs = []
    for i in range(count):
        for r in range(both):
            if i in (0, count - 1):
                pairs.append((i * both + r, i * both + (r ^ 1)))
            else:
                pairs.append((i * both + r, (i + 1 if i % 2 else i - 1) * both + r))
    return lax.ppermute(value, (axis, "rep"), pairs)


def to_partner(value, axis, s):
    count = lax.axis_size(axis)
    return lax.ppermute(value, axis, [(i, i ^ s) for i in range(count)])


def tree_sum(values):
    values = [v.astype(F32) for v in values]
    while len(values) > 1:
        values = [values[n] + values[n + 1] for n in range(0, len(values), 2)]
    return values[0]


def per_device(volume, first_kernel, first_bias, second_kernel, second_bias, cotangent):
    source = volume[0]
    cotan = cotangent[0, :, 0]
    n_sy, n_sx = lax.axis_size("sy"), lax.axis_size("sx")
    sx, sy, rep = (lax.axis_index(a) for a in ("sx", "sy", "rep"))
    odd_x = (sx % 2).astype(jnp.int32)
    odd_y = (sy % 2).astype(jnp.int32)
    cin, planes, rows, width = source.shape
    nf, rows2, width2 = cotan.shape
    c1 = first_kernel.shape[0]
    c2 = nf * n_sy
    own2 = rows // 2
    pairs = 14
    scale = 1.0 / math.sqrt(
        lax.axis_size("rep") * n_sx * n_sy * (planes // 2) * own2 * (width // 2)
    )
    me = sy.astype(jnp.int32).reshape(1)
    place = jnp.stack(
        [
            jnp.asarray(v, jnp.int32)
            for v in (odd_x, sy > 0, sy < n_sy - 1, sx, rep, (sx > 0) & (sx < n_sx - 1))
        ]
    )
    rim = 3

    w1 = first_kernel.transpose(2, 3, 4, 1, 0)
    w1q = jnp.concatenate(
        [
            jnp.pad(w1, ((0, 0), (0, 0), (0, 1), (0, 0), (0, 0))),
            jnp.pad(w1, ((0, 0), (0, 0), (1, 0), (0, 0), (0, 0))),
        ],
        axis=-1,
    )
    bias4 = jnp.tile(first_bias, 4)[:, None]
    w2 = second_kernel.transpose(2, 3, 4, 0, 1).reshape(27, nf, c1)
    vt = call(
        volume_body,
        "volume_cells",
        jax.ShapeDtypeStruct((planes, rows, cin, width), BF),
        [],
        (source,),
        flops=1 << 30,
    )
    cp, w2p = call(
        prep_body,
        "cotangent_cells",
        [
            jax.ShapeDtypeStruct((n_sy, own2 + 2, nf, width2), BF),
            jax.ShapeDtypeStruct((pairs, nf, 2 * c1), BF),
        ],
        [
            pltpu.VMEM((rows2 + 2, nf, width2), BF),
        ],
        (me, cotan, w2),
        smem_ins=1,
        flops=1 << 30,
    )

    edge_lo, edge_hi = vt[:, :rim], vt[:, rows - rim :]
    ya = swap_first(jnp.where(odd_y == 1, edge_lo, edge_hi), "sy")
    yb = swap_second(jnp.where(odd_y == 1, edge_hi, edge_lo), "sy")
    yb = jnp.where((sy > 0) & (sy < n_sy - 1), yb, jnp.zeros_like(yb))
    rim_lo = jnp.where(odd_y == 1, ya, yb)
    rim_hi = jnp.where(odd_y == 1, yb, ya)
    vr = jnp.concatenate([rim_lo, vt, rim_hi], axis=1)
    za = swap_first(jnp.where(odd_x == 1, vr[0], vr[planes - 1]), "sx")
    zb = swap_second(jnp.where(odd_x == 1, vr[planes - 1], vr[0]), "sx")

    cgot = [cp[0]] + [to_partner(cp[s], "sy", s) for s in range(1, n_sy)]
    w2p, vr = lax.optimization_barrier((w2p, vr))
    wgot = [w2p] + [to_partner(w2p, "sy", s) for s in range(1, n_sy)]

    pooled_rows = own2 + 2
    cell_shape = (rows + 2 * rim, 4 * cin, width // 2)
    cells, w1b, acc = call(
        conv1_own_body,
        "conv1_own",
        [
            jax.ShapeDtypeStruct((planes, *cell_shape), BF),
            jax.ShapeDtypeStruct((3, 4 * c1, 16 * cin), BF),
            jax.ShapeDtypeStruct((2, pooled_rows // 2, 4 * c1, width), F32),
        ],
        [],
        (vr, w1q, bias4),
        flops=2 << 30,
    )
    cgot, acc = lax.optimization_barrier((cgot, acc))
    co = jnp.stack(cgot)
    ca = swap_first(co, "sx")
    cb = swap_second(co, "sx")
    low, high, mask, pooled = call(
        conv1_body,
        "conv1",
        [
            jax.ShapeDtypeStruct(cell_shape, BF),
            jax.ShapeDtypeStruct(cell_shape, BF),
            jax.ShapeDtypeStruct((2, own2, 4 * c1, width // 2), BF),
            jax.ShapeDtypeStruct((pooled_rows, c1, width // 2), BF),
        ],
        [],
        (place, za, zb, w1b, acc),
        smem_ins=1,
        flops=1 << 30,
    )
    wgot, pooled = lax.optimization_barrier((wgot, pooled))
    w2r = jnp.stack(wgot)
    ua = swap_first(pooled, "sx")
    ub = swap_second(pooled, "sx")

    plane_shape = (own2 + 2, 3, c2, width2)
    wb, own_back, own_g2, own_b2 = call(
        own_body,
        "backward_own",
        [
            jax.ShapeDtypeStruct((3, c1, 9 * c2), BF),
            jax.ShapeDtypeStruct((own2 // 2, c1, 2 * width2), F32),
            jax.ShapeDtypeStruct((9, c2, 2 * c1), F32),
            jax.ShapeDtypeStruct((c2, 2 * c1), F32),
        ],
        [pltpu.VMEM(plane_shape, BF)],
        (co, pooled, w2r),
        flops=2 << 30,
    )
    hp = pairs // 2
    half_shape = jax.ShapeDtypeStruct((hp, c2 + cin, 2 * c1), F32)
    gp, back_g2, bias1 = call(
        back_body,
        "backward",
        [
            jax.ShapeDtypeStruct((2, own2 // 2, 4 * c1, width), BF),
            jax.ShapeDtypeStruct((2, 9, c2, 2 * c1), F32),
            jax.ShapeDtypeStruct((8, 4 * c1), F32),
        ],
        [pltpu.VMEM(plane_shape, BF), pltpu.VMEM(plane_shape, BF)],
        (place, mask, pooled, ca, cb, wb, own_back),
        smem_ins=1,
        flops=2 << 30,
    )
    gp, ua, ub = lax.optimization_barrier((gp, ua, ub))
    keep, send = call(
        weights_body,
        "first_weights",
        [half_shape, half_shape],
        [pltpu.VMEM((pairs, c2 + cin, 2 * c1), F32)],
        (place, cells, low, high, gp, back_g2, bias1, own_g2, own_b2),
        smem_ins=1,
        flops=3 << 30,
    )

    half = keep + swap_first(send, "rep")
    half, ua, ub = lax.optimization_barrier((half, ua, ub))
    half_bf = half.astype(BF)
    tail = half_bf[:, c2:]
    got = [
        to_partner(
            jnp.concatenate([half_bf[:, s * nf : (s + 1) * nf], tail], axis=1), "sy", s
        ).astype(F32)
        for s in range(1, n_sy)
    ]
    pieces = call(
        conv2_body,
        "conv2",
        jax.ShapeDtypeStruct((n_sy, own2, nf, width2), BF),
        [pltpu.VMEM((3, own2 + 2, 3, c1, width2), BF)],
        (place, pooled, ua, ub, w2r),
        smem_ins=1,
        flops=1 << 30,
    )
    own = jnp.concatenate([half[:, :nf], tail.astype(F32)], axis=1)
    part = tree_sum([own] + got).astype(BF)
    part, pieces = lax.optimization_barrier((part, pieces))
    parts = [part] + [to_partner(part, "sx", s) for s in range(1, n_sx)]
    flat = pieces.reshape(n_sy, own2 * nf, width2)
    out_got = [flat[0]] + [to_partner(flat[s], "sy", s) for s in range(1, n_sy)]
    bias_wide = jnp.broadcast_to(second_bias[:, None, None], (nf, 1, width2))
    second_out = call(
        unpack_body,
        "unpack",
        jax.ShapeDtypeStruct((nf, rows2, width2), F32),
        [],
        (me, *out_got, bias_wide),
        smem_ins=1,
        flops=1 << 28,
    )
    parts, second_out = lax.optimization_barrier((parts, second_out))
    total = tree_sum(parts) * scale
    other = swap_first(total, "rep")
    g2, t2, g1, t1 = call(
        finish_body,
        "finish",
        [
            jax.ShapeDtypeStruct((27, nf, c1), F32),
            jax.ShapeDtypeStruct((1, nf), F32),
            jax.ShapeDtypeStruct((27, cin, c1), F32),
            jax.ShapeDtypeStruct((1, c1), F32),
        ],
        [],
        (place, total, other),
        smem_ins=1,
        flops=1 << 20,
    )
    return (
        second_out[None, :, None],
        g1.reshape(3, 3, 3, cin, c1).transpose(4, 3, 0, 1, 2),
        t1[0],
        g2.reshape(3, 3, 3, nf, c1).transpose(3, 4, 0, 1, 2),
        t2[0],
    )


def solution(mesh):
    placed = (
        P("rep", None, "sx", "sy", None),
        P(),
        P(),
        P("sy", None, None, None, None),
        P("sy"),
        P("rep", "sy", "sx", None, None),
    )
    return jax.shard_map(
        per_device,
        mesh=mesh,
        in_specs=placed,
        out_specs=(
            P("rep", "sy", "sx", None, None),
            P(),
            P(),
            P("sy", None, None, None, None),
            P("sy"),
        ),
        check_vma=False,
    )
```

```python
import math

import jax
import jax.numpy as jnp
from jax import lax
from jax.experimental import pallas as pl
from jax.experimental.pallas import tpu as pltpu
from jax.sharding import PartitionSpec as P

BF = jnp.bfloat16
F32 = jnp.float32


def dot(a, b):
    return jnp.dot(a, b, preferred_element_type=F32)


def dot_nt(a, b):
    return lax.dot_general(a, b, (((1,), (1,)), ((), ())), preferred_element_type=F32)


def index_pair(rows, cols):
    shape = (rows, cols)
    return (
        lax.broadcasted_iota(jnp.int32, shape, 0),
        lax.broadcasted_iota(jnp.int32, shape, 1),
    )


def one_where(cond):
    return jnp.where(cond, 1.0, 0.0).astype(BF)


def swap_majors(outer, inner):
    r, c = index_pair(outer * inner, outer * inner)
    return one_where(lax.rem(r, outer) * inner + lax.div(r, outer) == c)


def shift_both(width):
    r, c = index_pair(width, 2 * width)
    return one_where(((c < width) & (r == c - 1)) | ((c >= width) & (r == c - width + 1)))


def identity(size):
    r, c = index_pair(size, size)
    return one_where(r == c)


def beside(place, below, first, second):
    use_first = jnp.where((place[0] == 1) == below, 1.0, 0.0)
    use_second = (1.0 - use_first) * jnp.where(place[2] == 1, 1.0, 0.0)
    lanes = (1, first.shape[-1])
    return first[...] * jnp.full(lanes, use_first, F32).astype(BF) + second[...] * jnp.full(
        lanes, use_second, F32
    ).astype(BF)


def call(body, name, outs, scratch, ins, smem_ins=0, flops=0, room=40):
    vm = pl.BlockSpec(memory_space=pltpu.VMEM)
    sm = pl.BlockSpec(memory_space=pltpu.SMEM)
    return pl.pallas_call(
        body,
        name=name,
        out_shape=outs,
        in_specs=[sm] * smem_ins + [vm] * (len(ins) - smem_ins),
        out_specs=jax.tree.map(lambda _: vm, outs),
        scratch_shapes=scratch,
        compiler_params=pltpu.CompilerParams(vmem_limit_bytes=room << 20),
        cost_estimate=pl.CostEstimate(flops=flops, bytes_accessed=1 << 20, transcendentals=0),
    )(*ins)


def volume_body(vol, vt):
    planes, rows, cin, width = vt.shape
    swap = swap_majors(cin, rows)
    half = width // 2
    r, c = index_pair(width, width)
    split = one_where(r == 2 * lax.rem(c, half) + lax.div(c, half))
    for x in range(planes):
        cells = dot(swap, vol[:, x].reshape(cin * rows, width)).astype(BF)
        vt[x] = dot(cells, split).astype(BF).reshape(rows, cin, width)


def prep_body(me, cot, w2, cp, w2p, cpad):
    nf, rows2, width2 = cot.shape
    step = 16
    swap2 = swap_majors(nf, step)
    for h in range(0, rows2, step):
        got = dot(swap2, cot[:, h : h + step].reshape(nf * step, width2))
        cpad[1 + h : 1 + h + step] = got.astype(BF).reshape(step, nf, width2)
    zero = jnp.zeros((1, nf, width2), BF)
    cpad[0:1] = zero
    cpad[rows2 + 1 : rows2 + 2] = zero
    count, rim_rows = cp.shape[0], cp.shape[1]
    for s in range(count):
        cp[s] = cpad[pl.ds((me[0] ^ s) * (rim_rows - 2), rim_rows)]
    taps, _, c1 = w2.shape
    pairs = w2p.shape[0]
    r, c = index_pair(c1, 2 * c1)
    low = dot(w2[:pairs].reshape(pairs * nf, c1), one_where(r == c))
    high = dot(w2[pairs:].reshape((taps - pairs) * nf, c1), one_where(r + c1 == c))
    for p in range(pairs):
        both = low[p * nf : (p + 1) * nf]
        if p + pairs < taps:
            both = both + high[p * nf : (p + 1) * nf]
        w2p[p] = both.astype(BF)


def moved_by_one(width):
    half = width // 2
    r, c = index_pair(width, width)
    return one_where(
        ((c < half) & (c > 0) & (r == half + c - 1))
        | ((c >= half) & (r == c - half + 1) & (r < half))
    )


def fill_cells(cells, plane, moved):
    rows, cin, width = plane.shape
    half = width // 2
    out = dot(plane.reshape(rows * cin, width), moved).astype(BF).reshape(rows, cin, width)
    cells[:, 0:cin] = out[:, :, :half]
    cells[:, cin : 2 * cin] = plane[:, :, :half]
    cells[:, 2 * cin : 3 * cin] = plane[:, :, half:]
    cells[:, 3 * cin : 4 * cin] = out[:, :, half:]


def two_rows(cells, first):
    rows, deep, half = cells.shape
    return jnp.concatenate(
        [cells[first + 2 * n : first + 2 * n + 4].reshape(4 * deep, half) for n in range(2)],
        axis=1,
    )


def conv1_own_body(vr, w1q, bias, cells, w1b, acc):
    planes, rows, cin, width = vr.shape
    c1 = bias.shape[0] // 4
    eye = identity(4 * c1)
    nothing = jnp.zeros((cin, 2 * c1), BF)
    for i in range(3):
        blocks = []
        for ys in range(4):
            for slot in range(4):
                left = w1q[i, ys, slot] if ys < 3 else nothing
                right = w1q[i, ys - 1, slot] if ys > 0 else nothing
                blocks.append(jnp.concatenate([left, right], axis=1))
        w1b[i] = dot_nt(eye, jnp.concatenate(blocks, axis=0)).astype(BF)
    moved = moved_by_one(width)
    for x in range(planes):
        fill_cells(cells.at[x], vr[x], moved)
    for t in range(acc.shape[1]):
        for xp in range(2):
            acc[xp, t] = (
                dot(w1b[1 - xp], two_rows(cells.at[0], 4 * t))
                + dot(w1b[2 - xp], two_rows(cells.at[1], 4 * t))
                + bias[...]
            )


def conv1_body(place, za, zb, w1b, acc, low, high, mask, pooled):
    rows, cin, width = za.shape
    half = width // 2
    c1 = pooled.shape[1]
    moved = moved_by_one(width)
    fill_cells(low, beside(place, True, za, zb), moved)
    fill_cells(high, beside(place, False, za, zb), moved)
    rows2 = pooled.shape[0]
    for t in range(rows2 // 2):
        total = None
        for xp, cells in ((0, low), (1, high)):
            pre = acc[xp, t] + dot(w1b[2 * xp], two_rows(cells, 4 * t))
            above = pre > 0
            flags = jnp.where(above, 1.0, 0.0).astype(BF)
            mask[xp, 2 * t] = flags[:, :half]
            mask[xp, 2 * t + 1] = flags[:, half:]
            act = jnp.where(above, pre, 0.3 * pre)
            for b in range(4):
                piece = act[b * c1 : (b + 1) * c1]
                total = piece if total is None else total + piece
        mean = (total * 0.125).astype(BF)
        pooled[2 * t] = mean[:, :half]
        pooled[2 * t + 1] = mean[:, half:]


def with_shifts(store, plane, shifts):
    rows, chans, width = plane.shape
    out = dot(plane.reshape(rows * chans, width), shifts).astype(BF).reshape(rows, chans, 2 * width)
    store(0, out[:, :, :width])
    store(1, plane)
    store(2, out[:, :, width:])


def conv2_body(place, ur, ua, ub, w2r, pieces, u):
    rows, c1, width = ur.shape
    count, pairs, nf, _ = w2r.shape
    shifts = shift_both(width)
    planes = (beside(place, True, ua, ub), ur[...], beside(place, False, ua, ub))
    for x in range(3):

        def store(k, value, x=x):
            u[x, :, k] = value

        with_shifts(store, planes[x], shifts)
    weights = jnp.concatenate(
        [jnp.concatenate([w2r[s, p] for s in range(count)], axis=0) for p in range(pairs)], axis=1
    )

    def tap(y, d):
        d = d if d < 27 else 0
        return u[d // 9, y + (d // 3) % 3, d % 3]

    def deep(y):
        return jnp.concatenate(
            [tap(y, d) for p in range(pairs) for d in (p, p + pairs)], axis=0
        )

    for y in range(0, rows - 2, 2):
        rhs = jnp.concatenate([deep(y), deep(y + 1)], axis=1)
        out = dot(weights, rhs).astype(BF)
        for s in range(count):
            pieces[s, y] = out[s * nf : (s + 1) * nf, :width]
            pieces[s, y + 1] = out[s * nf : (s + 1) * nf, width:]


def block_taps(block):
    if block < 9:
        return block * 3, block * 3 + 1
    first = 2 * (block - 9)
    return first * 3 + 2, (first + 1) * 3 + 2 if first < 8 else 27


def fill_plane(t_ref, plane):
    for s in range(plane.shape[0]):
        nf = plane.shape[2]
        t_ref[:, s * nf : (s + 1) * nf] = plane[s]


def pair_rows(t_ref, t):
    rows, chans, width = t_ref.shape
    return jnp.concatenate(
        [t_ref[2 * t + n : 2 * t + n + 3].reshape(3 * chans, width) for n in range(2)], axis=1
    )


def rows_wide(t_ref):
    count = t_ref.shape[0] - 2
    return jnp.concatenate(
        [
            jnp.concatenate([t_ref[y + ys] for y in range(count)], axis=1)
            for ys in range(3)
        ],
        axis=0,
    )


def own_body(co, pooled, w2r, wb, wide, own_back, own_g2, own_b2, t_ref):
    count, rows, nf, width = co.shape
    pairs = w2r.shape[1]
    c1 = pooled.shape[1]
    c2 = count * nf
    fill_plane(t_ref, co)
    eye = identity(2 * c1)
    for p in range(pairs):
        block = jnp.concatenate([w2r[s, p] for s in range(count)], axis=0)
        turned = dot_nt(eye, block).astype(BF)
        for half, d in ((0, p), (1, p + pairs)):
            if d < 27:
                i, j, k = d // 9, (d // 3) % 3, d % 3
                at = (2 - j) * c2
                wb[2 - i, k * c1 : (k + 1) * c1, at : at + c2] = turned[
                    half * c1 : (half + 1) * c1
                ]
    for t in range((rows - 2) // 2):
        own_back[t] = dot(wb[1], pair_rows(t_ref, t))
    cells2 = pooled.shape[0]
    moved = dot(pooled[...].reshape(cells2 * c1, width), shift_both(width)).astype(BF)
    for y in range(cells2):
        lanes = slice(y * width, (y + 1) * width)
        after = moved[y * c1 : (y + 1) * c1, width:]
        wide[0:c1, lanes] = moved[y * c1 : (y + 1) * c1, :width]
        wide[c1 : 2 * c1, lanes] = pooled[y]
        wide[2 * c1 : 3 * c1, lanes] = after
        wide[3 * c1 : 4 * c1, lanes] = after
    own_g2[...] = dot_nt(rows_wide(t_ref), wide[...])
    sums = None
    for y in range(1, rows - 1):
        v = t_ref[y].astype(F32)
        sums = v if sums is None else sums + v
    own_b2[...] = jnp.broadcast_to(jnp.sum(sums, axis=1, keepdims=True), own_b2.shape)


def back_body(place, mask, wide, ca, cb, wb, own_back, gp, g2, bias1, t0, t2):
    count, rows, nf, width = ca.shape
    c1 = wide.shape[0] // 4
    fill_plane(t0, beside(place, True, ca, cb))
    fill_plane(t2, beside(place, False, ca, cb))
    sums = jnp.zeros((8, 4 * c1), F32)
    ones = jnp.ones((8, 2 * width), BF)
    lane = lax.broadcasted_iota(jnp.int32, (c1, width), 1)
    for t in range((rows - 2) // 2):
        acc = own_back[t] + dot(wb[0], pair_rows(t0, t)) + dot(wb[2], pair_rows(t2, t))
        rows_back = []
        for n in range(2):
            part = acc[:, n * width : (n + 1) * width]
            ahead = pltpu.roll(part[:c1], width - 1, 1)
            behind = pltpu.roll(part[2 * c1 :], 1, 1)
            rows_back.append(
                part[c1 : 2 * c1]
                + jnp.where(lane < width - 1, ahead, 0.0)
                + jnp.where(lane > 0, behind, 0.0)
            )
        eighth = jnp.concatenate(rows_back, axis=1) * 0.125
        spread = jnp.concatenate([eighth] * 4, axis=0)
        for xp in range(2):
            flags = jnp.concatenate([mask[xp, 2 * t], mask[xp, 2 * t + 1]], axis=1)
            grad = (spread * jnp.where(flags > 0, 1.0, 0.3)).astype(BF)
            gp[xp, t] = grad
            sums = sums + dot_nt(ones, grad)
    bias1[...] = sums
    g2[0] = dot_nt(rows_wide(t0), wide[...])
    g2[1] = dot_nt(rows_wide(t2), wide[...])


def weights_body(place, cells, low, high, gp, g2, bias1, own_g2, own_b2, keep, send, red):
    c2, wide_lanes = own_b2.shape
    c1 = wide_lanes // 2
    cin = cells.shape[2] // 4
    n_pairs = gp.shape[1]
    pairs = 14
    sources = (low, cells.at[0], cells.at[1], high)

    def part2(ij):
        x, ys = 2 - ij // 3, 2 - ij % 3
        rows_of = slice(ys * c2, (ys + 1) * c2)
        return own_g2[rows_of] if x == 1 else g2[x // 2, rows_of]

    low_wide = lax.broadcasted_iota(jnp.int32, (c2, 2 * c1), 1) < c1
    for ij in range(9):
        red[ij, :c2] = part2(ij)[:, : 2 * c1]
    for m in range(5):
        other = part2(2 * m + 1)[:, 2 * c1 :] if m < 4 else own_b2[...]
        red[9 + m, :c2] = jnp.where(low_wide, part2(2 * m)[:, 2 * c1 :], other)
    lane = lax.broadcasted_iota(jnp.int32, (cin, 2 * c1), 1)
    low_half = lane < c1
    lows, highs = {}, {}
    for i in range(3):
        acc = None
        for xp in range(2):
            for t in range(n_pairs):
                lhs = two_rows(sources[xp + i], 4 * t)
                part = dot_nt(lhs, gp[xp, t])
                acc = part if acc is None else acc + part
        for j in range(3):
            slots = []
            for slot in range(4):
                r0 = (j * 4 + slot) * cin
                r1 = ((j + 1) * 4 + slot) * cin
                slots.append(acc[r0 : r0 + cin, : 2 * c1] + acc[r1 : r1 + cin, 2 * c1 :])
            turned = [pltpu.roll(v, c1, 1) for v in slots]
            n = i * 3 + j
            red[n, c2:] = jnp.where(low_half, slots[0], slots[2]) + turned[1]
            lows[n] = slots[2] + turned[3]
            highs[n] = slots[3] + turned[2]
    b1 = bias1[:, : 2 * c1] + bias1[:, 2 * c1 :]
    b1 = b1 + pltpu.roll(b1, c1, 1)
    highs[9] = jnp.concatenate([b1] * (cin // 8), axis=0)
    for m in range(5):
        red[9 + m, c2:] = jnp.where(low_half, lows[2 * m], highs[2 * m + 1])
    hp = pairs // 2
    keep[...] = red[pl.ds(place[1] * hp, hp)]
    send[...] = red[pl.ds((1 - place[1]) * hp, hp)]


def unpack_body(me, *refs):
    pieces, bias, out = refs[:-2], refs[-2], refs[-1]
    nf, _, width = bias.shape
    rows = out.shape[1] // len(pieces)
    swap = swap_majors(rows, nf)
    for s, piece in enumerate(pieces):
        got = dot(swap, piece[: rows * nf]).reshape(nf, rows, width)
        out[:, pl.ds(pl.multiple_of((me[0] ^ s) * rows, rows), rows), :] = got + bias[...]


def finish_body(place, mine, other, g2, b2, g1, b1):
    hp, _, width = mine.shape
    nf, c1 = g2.shape[1], g2.shape[2]
    first = place[1] == 0
    got, more = mine[...], other[...]
    halves = (jnp.where(first, got, more), jnp.where(first, more, got))
    for p in range(2 * hp):
        block = halves[p // hp][p % hp]
        turned = pltpu.roll(block, c1, 1)
        for d, v in zip(block_taps(p), (block, turned)):
            low, high = v[:nf, :c1], v[nf:, :c1]
            if d < 27:
                g2[d] = low
                g1[d] = high
            else:
                column = lax.broadcasted_iota(jnp.int32, low.shape, 0)
                lane = lax.broadcasted_iota(jnp.int32, low.shape, 1)
                row = jnp.sum(jnp.where(column == lane, low, 0.0), axis=0, keepdims=True)
                b2[...] = row[:, :nf]
                b1[...] = high[0:1]


def swap_first(value, axis):
    count = lax.axis_size(axis)
    return lax.ppermute(value, axis, [(i, i ^ 1) for i in range(count)])


def swap_second(value, axis):
    count = lax.axis_size(axis)
    both = lax.axis_size("rep")
    pairs = []
    for i in range(count):
        for r in range(both):
            if i in (0, count - 1):
                pairs.append((i * both + r, i * both + (r ^ 1)))
            else:
                pairs.append((i * both + r, (i + 1 if i % 2 else i - 1) * both + r))
    return lax.ppermute(value, (axis, "rep"), pairs)


def to_partner(value, axis, s):
    count = lax.axis_size(axis)
    return lax.ppermute(value, axis, [(i, i ^ s) for i in range(count)])


def tree_sum(values):
    values = [v.astype(F32) for v in values]
    while len(values) > 1:
        values = [values[n] + values[n + 1] for n in range(0, len(values), 2)]
    return values[0]


def per_device(volume, first_kernel, first_bias, second_kernel, second_bias, cotangent):
    source = volume[0]
    cotan = cotangent[0, :, 0]
    n_sy, n_sx = lax.axis_size("sy"), lax.axis_size("sx")
    sx, sy, rep = (lax.axis_index(a) for a in ("sx", "sy", "rep"))
    odd_x = (sx % 2).astype(jnp.int32)
    odd_y = (sy % 2).astype(jnp.int32)
    cin, planes, rows, width = source.shape
    nf, rows2, width2 = cotan.shape
    c1 = first_kernel.shape[0]
    c2 = nf * n_sy
    own2 = rows // 2
    pairs = 14
    scale = 1.0 / math.sqrt(
        lax.axis_size("rep") * n_sx * n_sy * (planes // 2) * own2 * (width // 2)
    )
    me = sy.astype(jnp.int32).reshape(1)
    place = jnp.stack(
        [
            jnp.asarray(v, jnp.int32)
            for v in (odd_x, rep, (sx > 0) & (sx < n_sx - 1))
        ]
    )
    rim = 1

    w1 = first_kernel.transpose(2, 3, 4, 1, 0)
    w1q = jnp.concatenate(
        [
            jnp.pad(w1, ((0, 0), (0, 0), (0, 1), (0, 0), (0, 0))),
            jnp.pad(w1, ((0, 0), (0, 0), (1, 0), (0, 0), (0, 0))),
        ],
        axis=-1,
    )
    bias4 = jnp.tile(first_bias, 4)[:, None]
    w2 = second_kernel.transpose(2, 3, 4, 0, 1).reshape(27, nf, c1)
    vt = call(
        volume_body,
        "volume_cells",
        jax.ShapeDtypeStruct((planes, rows, cin, width), BF),
        [],
        (source,),
        flops=1 << 30,
    )
    cp, w2p = call(
        prep_body,
        "cotangent_cells",
        [
            jax.ShapeDtypeStruct((n_sy, own2 + 2, nf, width2), BF),
            jax.ShapeDtypeStruct((pairs, nf, 2 * c1), BF),
        ],
        [
            pltpu.VMEM((rows2 + 2, nf, width2), BF),
        ],
        (me, cotan, w2),
        smem_ins=1,
        flops=1 << 30,
    )

    edge_lo, edge_hi = vt[:, :rim], vt[:, rows - rim :]
    ya = swap_first(jnp.where(odd_y == 1, edge_lo, edge_hi), "sy")
    yb = swap_second(jnp.where(odd_y == 1, edge_hi, edge_lo), "sy")
    yb = jnp.where((sy > 0) & (sy < n_sy - 1), yb, jnp.zeros_like(yb))
    rim_lo = jnp.where(odd_y == 1, ya, yb)
    rim_hi = jnp.where(odd_y == 1, yb, ya)
    vr = jnp.concatenate([rim_lo, vt, rim_hi], axis=1)
    za = swap_first(jnp.where(odd_x == 1, vr[0], vr[planes - 1]), "sx")
    zb = swap_second(jnp.where(odd_x == 1, vr[planes - 1], vr[0]), "sx")

    cgot = [cp[0]] + [to_partner(cp[s], "sy", s) for s in range(1, n_sy)]
    w2p, vr = lax.optimization_barrier((w2p, vr))
    wgot = [w2p] + [to_partner(w2p, "sy", s) for s in range(1, n_sy)]

    pooled_rows = own2
    cell_shape = (rows + 2 * rim, 4 * cin, width // 2)
    cells, w1b, acc = call(
        conv1_own_body,
        "conv1_own",
        [
            jax.ShapeDtypeStruct((planes, *cell_shape), BF),
            jax.ShapeDtypeStruct((3, 4 * c1, 16 * cin), BF),
            jax.ShapeDtypeStruct((2, pooled_rows // 2, 4 * c1, width), F32),
        ],
        [],
        (vr, w1q, bias4),
        flops=2 << 30,
    )
    cgot, acc = lax.optimization_barrier((cgot, acc))
    co = jnp.stack(cgot)
    ca = swap_first(co, "sx")
    cb = swap_second(co, "sx")
    low, high, mask, pooled = call(
        conv1_body,
        "conv1",
        [
            jax.ShapeDtypeStruct(cell_shape, BF),
            jax.ShapeDtypeStruct(cell_shape, BF),
            jax.ShapeDtypeStruct((2, own2, 4 * c1, width // 2), BF),
            jax.ShapeDtypeStruct((pooled_rows, c1, width // 2), BF),
        ],
        [],
        (place, za, zb, w1b, acc),
        smem_ins=1,
        flops=1 << 30,
    )
    wgot, _ = lax.optimization_barrier((wgot, pooled))
    w2r = jnp.stack(wgot)
    pa = swap_first(jnp.where(odd_y == 1, pooled[0], pooled[own2 - 1]), "sy")
    pb = swap_second(jnp.where(odd_y == 1, pooled[own2 - 1], pooled[0]), "sy")
    pb = jnp.where((sy > 0) & (sy < n_sy - 1), pb, jnp.zeros_like(pb))
    ur = jnp.concatenate(
        [
            jnp.where(odd_y == 1, pa, pb)[None],
            pooled,
            jnp.where(odd_y == 1, pb, pa)[None],
        ],
        axis=0,
    )
    ua = swap_first(ur, "sx")
    ub = swap_second(ur, "sx")

    plane_shape = (own2 + 2, c2, width2)
    wb, wide, own_back, own_g2, own_b2 = call(
        own_body,
        "backward_own",
        [
            jax.ShapeDtypeStruct((3, 3 * c1, 3 * c2), BF),
            jax.ShapeDtypeStruct((4 * c1, own2 * width2), BF),
            jax.ShapeDtypeStruct((own2 // 2, 3 * c1, 2 * width2), F32),
            jax.ShapeDtypeStruct((3 * c2, 4 * c1), F32),
            jax.ShapeDtypeStruct((c2, 2 * c1), F32),
        ],
        [pltpu.VMEM(plane_shape, BF)],
        (co, pooled, w2r),
        flops=2 << 30,
    )
    hp = pairs // 2
    half_shape = jax.ShapeDtypeStruct((hp, c2 + cin, 2 * c1), F32)
    gp, back_g2, bias1 = call(
        back_body,
        "backward",
        [
            jax.ShapeDtypeStruct((2, own2 // 2, 4 * c1, width), BF),
            jax.ShapeDtypeStruct((2, 3 * c2, 4 * c1), F32),
            jax.ShapeDtypeStruct((8, 4 * c1), F32),
        ],
        [pltpu.VMEM(plane_shape, BF), pltpu.VMEM(plane_shape, BF)],
        (place, mask, wide, ca, cb, wb, own_back),
        smem_ins=1,
        flops=2 << 30,
    )
    keep, send = call(
        weights_body,
        "first_weights",
        [half_shape, half_shape],
        [pltpu.VMEM((pairs, c2 + cin, 2 * c1), F32)],
        (place, cells, low, high, gp, back_g2, bias1, own_g2, own_b2),
        smem_ins=1,
        flops=3 << 30,
    )

    send, ua, ub = lax.optimization_barrier((send, ua, ub))
    half = keep + swap_first(send, "rep")
    half, ua, ub = lax.optimization_barrier((half, ua, ub))
    half_bf = half.astype(BF)
    tail = half_bf[:, c2:]
    got = [
        to_partner(
            jnp.concatenate([half_bf[:, s * nf : (s + 1) * nf], tail], axis=1), "sy", s
        ).astype(F32)
        for s in range(1, n_sy)
    ]
    pieces = call(
        conv2_body,
        "conv2",
        jax.ShapeDtypeStruct((n_sy, own2, nf, width2), BF),
        [pltpu.VMEM((3, own2 + 2, 3, c1, width2), BF)],
        (place, ur, ua, ub, w2r),
        smem_ins=1,
        flops=1 << 30,
    )
    own = jnp.concatenate([half[:, :nf], tail.astype(F32)], axis=1)
    flat = pieces.reshape(n_sy, own2 * nf, width2)
    beside_sy = to_partner(flat[1], "sy", 1)
    got, beside_sy = lax.optimization_barrier((got, beside_sy))
    part = tree_sum([own] + got).astype(BF)
    part, flat = lax.optimization_barrier((part, flat))
    parts = [part] + [to_partner(part, "sx", s) for s in range(1, n_sx)]
    out_got = [flat[0], beside_sy] + [to_partner(flat[s], "sy", s) for s in range(2, n_sy)]
    bias_wide = jnp.broadcast_to(second_bias[:, None, None], (nf, 1, width2))
    second_out = call(
        unpack_body,
        "unpack",
        jax.ShapeDtypeStruct((nf, rows2, width2), F32),
        [],
        (me, *out_got, bias_wide),
        smem_ins=1,
        flops=1 << 28,
    )
    parts, second_out = lax.optimization_barrier((parts, second_out))
    total = tree_sum(parts) * scale
    other = swap_first(total, "rep")
    g2, t2, g1, t1 = call(
        finish_body,
        "finish",
        [
            jax.ShapeDtypeStruct((27, nf, c1), F32),
            jax.ShapeDtypeStruct((1, nf), F32),
            jax.ShapeDtypeStruct((27, cin, c1), F32),
            jax.ShapeDtypeStruct((1, c1), F32),
        ],
        [],
        (place, total, other),
        smem_ins=1,
        flops=1 << 20,
    )
    return (
        second_out[None, :, None],
        g1.reshape(3, 3, 3, cin, c1).transpose(4, 3, 0, 1, 2),
        t1[0],
        g2.reshape(3, 3, 3, nf, c1).transpose(3, 4, 0, 1, 2),
        t2[0],
    )


def solution(mesh):
    placed = (
        P("rep", None, "sx", "sy", None),
        P(),
        P(),
        P("sy", None, None, None, None),
        P("sy"),
        P("rep", "sy", "sx", None, None),
    )
    return jax.shard_map(
        per_device,
        mesh=mesh,
        in_specs=placed,
        out_specs=(
            P("rep", "sy", "sx", None, None),
            P(),
            P(),
            P("sy", None, None, None, None),
            P("sy"),
        ),
        check_vma=False,
    )
```

```python
import math

import jax
import jax.numpy as jnp
from jax import lax
from jax.experimental import pallas as pl
from jax.experimental.pallas import tpu as pltpu
from jax.sharding import PartitionSpec as P

BF = jnp.bfloat16
F32 = jnp.float32


def dot(a, b):
    return jnp.dot(a, b, preferred_element_type=F32)


def dot_nt(a, b):
    return lax.dot_general(a, b, (((1,), (1,)), ((), ())), preferred_element_type=F32)


def index_pair(rows, cols):
    shape = (rows, cols)
    return (
        lax.broadcasted_iota(jnp.int32, shape, 0),
        lax.broadcasted_iota(jnp.int32, shape, 1),
    )


def one_where(cond):
    return jnp.where(cond, 1.0, 0.0).astype(BF)


def swap_majors(outer, inner):
    r, c = index_pair(outer * inner, outer * inner)
    return one_where(lax.rem(r, outer) * inner + lax.div(r, outer) == c)


def shift_both(width):
    r, c = index_pair(width, 2 * width)
    return one_where(((c < width) & (r == c - 1)) | ((c >= width) & (r == c - width + 1)))


def identity(size):
    r, c = index_pair(size, size)
    return one_where(r == c)


def beside(place, below, first, second):
    use_first = jnp.where((place[0] == 1) == below, 1.0, 0.0)
    use_second = (1.0 - use_first) * jnp.where(place[2] == 1, 1.0, 0.0)
    lanes = (1, first.shape[-1])
    return first[...] * jnp.full(lanes, use_first, F32).astype(BF) + second[...] * jnp.full(
        lanes, use_second, F32
    ).astype(BF)


def call(body, name, outs, scratch, ins, smem_ins=0, flops=0, room=40):
    vm = pl.BlockSpec(memory_space=pltpu.VMEM)
    sm = pl.BlockSpec(memory_space=pltpu.SMEM)
    return pl.pallas_call(
        body,
        name=name,
        out_shape=outs,
        in_specs=[sm] * smem_ins + [vm] * (len(ins) - smem_ins),
        out_specs=jax.tree.map(lambda _: vm, outs),
        scratch_shapes=scratch,
        compiler_params=pltpu.CompilerParams(vmem_limit_bytes=room << 20),
        cost_estimate=pl.CostEstimate(flops=flops, bytes_accessed=1 << 20, transcendentals=0),
    )(*ins)


def volume_body(vol, vt):
    planes, rows, cin, width = vt.shape
    swap = swap_majors(cin, rows)
    half = width // 2
    r, c = index_pair(width, width)
    split = one_where(r == 2 * lax.rem(c, half) + lax.div(c, half))
    for x in range(planes):
        cells = dot(swap, vol[:, x].reshape(cin * rows, width)).astype(BF)
        vt[x] = dot(cells, split).astype(BF).reshape(rows, cin, width)


def prep_body(me, cot, w2, cp, w2p, cpad):
    nf, rows2, width2 = cot.shape
    step = 16
    swap2 = swap_majors(nf, step)
    for h in range(0, rows2, step):
        got = dot(swap2, cot[:, h : h + step].reshape(nf * step, width2))
        cpad[1 + h : 1 + h + step] = got.astype(BF).reshape(step, nf, width2)
    zero = jnp.zeros((1, nf, width2), BF)
    cpad[0:1] = zero
    cpad[rows2 + 1 : rows2 + 2] = zero
    count, rim_rows = cp.shape[0], cp.shape[1]
    for s in range(count):
        cp[s] = cpad[pl.ds((me[0] ^ s) * (rim_rows - 2), rim_rows)]
    taps, _, c1 = w2.shape
    pairs = w2p.shape[0]
    r, c = index_pair(c1, 2 * c1)
    low = dot(w2[:pairs].reshape(pairs * nf, c1), one_where(r == c))
    high = dot(w2[pairs:].reshape((taps - pairs) * nf, c1), one_where(r + c1 == c))
    for p in range(pairs):
        both = low[p * nf : (p + 1) * nf]
        if p + pairs < taps:
            both = both + high[p * nf : (p + 1) * nf]
        w2p[p] = both.astype(BF)


def moved_by_one(width):
    half = width // 2
    r, c = index_pair(width, width)
    return one_where(
        ((c < half) & (c > 0) & (r == half + c - 1))
        | ((c >= half) & (r == c - half + 1) & (r < half))
    )


def fill_cells(cells, plane, moved):
    rows, cin, width = plane.shape
    half = width // 2
    out = dot(plane.reshape(rows * cin, width), moved).astype(BF).reshape(rows, cin, width)
    cells[:, 0:cin] = out[:, :, :half]
    cells[:, cin : 2 * cin] = plane[:, :, :half]
    cells[:, 2 * cin : 3 * cin] = plane[:, :, half:]
    cells[:, 3 * cin : 4 * cin] = out[:, :, half:]


def two_rows(cells, first):
    rows, deep, half = cells.shape
    return jnp.concatenate(
        [cells[first + 2 * n : first + 2 * n + 4].reshape(4 * deep, half) for n in range(2)],
        axis=1,
    )


def conv1_own_body(vr, w1q, bias, cells, w1b, acc):
    planes, rows, cin, width = vr.shape
    c1 = bias.shape[0] // 4
    eye = identity(4 * c1)
    nothing = jnp.zeros((cin, 2 * c1), BF)
    for i in range(3):
        blocks = []
        for ys in range(4):
            for slot in range(4):
                left = w1q[i, ys, slot] if ys < 3 else nothing
                right = w1q[i, ys - 1, slot] if ys > 0 else nothing
                blocks.append(jnp.concatenate([left, right], axis=1))
        w1b[i] = dot_nt(eye, jnp.concatenate(blocks, axis=0)).astype(BF)
    moved = moved_by_one(width)
    for x in range(planes):
        fill_cells(cells.at[x], vr[x], moved)
    for t in range(acc.shape[1]):
        for xp in range(2):
            acc[xp, t] = (
                dot(w1b[1 - xp], two_rows(cells.at[0], 4 * t))
                + dot(w1b[2 - xp], two_rows(cells.at[1], 4 * t))
                + bias[...]
            )


def conv1_body(place, za, zb, w1b, acc, low, high, mask, pooled):
    rows, cin, width = za.shape
    half = width // 2
    c1 = pooled.shape[1]
    moved = moved_by_one(width)
    fill_cells(low, beside(place, True, za, zb), moved)
    fill_cells(high, beside(place, False, za, zb), moved)
    rows2 = pooled.shape[0]
    for t in range(rows2 // 2):
        total = None
        for xp, cells in ((0, low), (1, high)):
            pre = acc[xp, t] + dot(w1b[2 * xp], two_rows(cells, 4 * t))
            above = pre > 0
            flags = jnp.where(above, 1.0, 0.0).astype(BF)
            mask[xp, 2 * t] = flags[:, :half]
            mask[xp, 2 * t + 1] = flags[:, half:]
            act = jnp.where(above, pre, 0.3 * pre)
            for b in range(4):
                piece = act[b * c1 : (b + 1) * c1]
                total = piece if total is None else total + piece
        mean = (total * 0.125).astype(BF)
        pooled[2 * t] = mean[:, :half]
        pooled[2 * t + 1] = mean[:, half:]


def with_shifts(store, plane, shifts):
    rows, chans, width = plane.shape
    out = dot(plane.reshape(rows * chans, width), shifts).astype(BF).reshape(rows, chans, 2 * width)
    store(0, out[:, :, :width])
    store(1, plane)
    store(2, out[:, :, width:])


def conv2_body(place, ur, ua, ub, w2r, pieces, u):
    rows, c1, width = ur.shape
    count, pairs, nf, _ = w2r.shape
    shifts = shift_both(width)
    planes = (beside(place, True, ua, ub), ur[...], beside(place, False, ua, ub))
    for x in range(3):

        def store(k, value, x=x):
            u[x, :, k] = value

        with_shifts(store, planes[x], shifts)
    weights = jnp.concatenate(
        [jnp.concatenate([w2r[s, p] for s in range(count)], axis=0) for p in range(pairs)], axis=1
    )

    def tap(y, d):
        d = d if d < 27 else 0
        return u[d // 9, y + (d // 3) % 3, d % 3]

    def deep(y):
        return jnp.concatenate(
            [tap(y, d) for p in range(pairs) for d in (p, p + pairs)], axis=0
        )

    for y in range(0, rows - 2, 2):
        rhs = jnp.concatenate([deep(y), deep(y + 1)], axis=1)
        out = dot(weights, rhs).astype(BF)
        for s in range(count):
            pieces[s, y] = out[s * nf : (s + 1) * nf, :width]
            pieces[s, y + 1] = out[s * nf : (s + 1) * nf, width:]


def block_taps(block):
    if block < 9:
        return block * 3, block * 3 + 1
    first = 2 * (block - 9)
    return first * 3 + 2, (first + 1) * 3 + 2 if first < 8 else 27


def fill_plane(t_ref, plane):
    for s in range(plane.shape[0]):
        nf = plane.shape[2]
        t_ref[:, s * nf : (s + 1) * nf] = plane[s]


def pair_rows(t_ref, t):
    rows, chans, width = t_ref.shape
    return jnp.concatenate(
        [t_ref[2 * t + n : 2 * t + n + 3].reshape(3 * chans, width) for n in range(2)], axis=1
    )


def rows_wide(t_ref):
    count = t_ref.shape[0] - 2
    return jnp.concatenate(
        [
            jnp.concatenate([t_ref[y + ys] for y in range(count)], axis=1)
            for ys in range(3)
        ],
        axis=0,
    )


def own_body(co, pooled, w2r, wb, wide, own_back, own_g2, own_b2, t_ref):
    count, rows, nf, width = co.shape
    pairs = w2r.shape[1]
    c1 = pooled.shape[1]
    c2 = count * nf
    fill_plane(t_ref, co)
    eye = identity(2 * c1)
    for p in range(pairs):
        block = jnp.concatenate([w2r[s, p] for s in range(count)], axis=0)
        turned = dot_nt(eye, block).astype(BF)
        for half, d in ((0, p), (1, p + pairs)):
            if d < 27:
                i, j, k = d // 9, (d // 3) % 3, d % 3
                at = (2 - j) * c2
                wb[2 - i, k * c1 : (k + 1) * c1, at : at + c2] = turned[
                    half * c1 : (half + 1) * c1
                ]
    for t in range((rows - 2) // 2):
        own_back[t] = dot(wb[1], pair_rows(t_ref, t))
    cells2 = pooled.shape[0]
    moved = dot(pooled[...].reshape(cells2 * c1, width), shift_both(width)).astype(BF)
    for y in range(cells2):
        lanes = slice(y * width, (y + 1) * width)
        after = moved[y * c1 : (y + 1) * c1, width:]
        wide[0:c1, lanes] = moved[y * c1 : (y + 1) * c1, :width]
        wide[c1 : 2 * c1, lanes] = pooled[y]
        wide[2 * c1 : 3 * c1, lanes] = after
        wide[3 * c1 : 4 * c1, lanes] = after
    own_g2[...] = dot_nt(rows_wide(t_ref), wide[...])
    sums = None
    for y in range(1, rows - 1):
        v = t_ref[y].astype(F32)
        sums = v if sums is None else sums + v
    own_b2[...] = jnp.broadcast_to(jnp.sum(sums, axis=1, keepdims=True), own_b2.shape)


def back_body(place, mask, wide, ca, cb, wb, own_back, gp, g2, bias1, t0, t2):
    count, rows, nf, width = ca.shape
    c1 = wide.shape[0] // 4
    fill_plane(t0, beside(place, True, ca, cb))
    fill_plane(t2, beside(place, False, ca, cb))
    sums = jnp.zeros((8, 4 * c1), F32)
    ones = jnp.ones((8, 2 * width), BF)
    lane = lax.broadcasted_iota(jnp.int32, (c1, width), 1)
    for t in range((rows - 2) // 2):
        acc = own_back[t] + dot(wb[0], pair_rows(t0, t)) + dot(wb[2], pair_rows(t2, t))
        rows_back = []
        for n in range(2):
            part = acc[:, n * width : (n + 1) * width]
            ahead = pltpu.roll(part[:c1], width - 1, 1)
            behind = pltpu.roll(part[2 * c1 :], 1, 1)
            rows_back.append(
                part[c1 : 2 * c1]
                + jnp.where(lane < width - 1, ahead, 0.0)
                + jnp.where(lane > 0, behind, 0.0)
            )
        eighth = jnp.concatenate(rows_back, axis=1) * 0.125
        spread = jnp.concatenate([eighth] * 4, axis=0)
        for xp in range(2):
            flags = jnp.concatenate([mask[xp, 2 * t], mask[xp, 2 * t + 1]], axis=1)
            grad = (spread * jnp.where(flags > 0, 1.0, 0.3)).astype(BF)
            gp[xp, t] = grad
            sums = sums + dot_nt(ones, grad)
    bias1[...] = sums
    g2[0] = dot_nt(rows_wide(t0), wide[...])
    g2[1] = dot_nt(rows_wide(t2), wide[...])


def weights_body(place, cells, low, high, gp, g2, bias1, own_g2, own_b2, keep, send, red):
    c2, wide_lanes = own_b2.shape
    c1 = wide_lanes // 2
    cin = cells.shape[2] // 4
    n_pairs = gp.shape[1]
    pairs = 14
    sources = (low, cells.at[0], cells.at[1], high)

    def part2(ij):
        x, ys = 2 - ij // 3, 2 - ij % 3
        rows_of = slice(ys * c2, (ys + 1) * c2)
        return own_g2[rows_of] if x == 1 else g2[x // 2, rows_of]

    low_wide = lax.broadcasted_iota(jnp.int32, (c2, 2 * c1), 1) < c1
    for ij in range(9):
        red[ij, :c2] = part2(ij)[:, : 2 * c1]
    for m in range(5):
        other = part2(2 * m + 1)[:, 2 * c1 :] if m < 4 else own_b2[...]
        red[9 + m, :c2] = jnp.where(low_wide, part2(2 * m)[:, 2 * c1 :], other)
    lane = lax.broadcasted_iota(jnp.int32, (cin, 2 * c1), 1)
    low_half = lane < c1
    lows, highs = {}, {}
    for i in range(3):
        acc = None
        for xp in range(2):
            for t in range(n_pairs):
                lhs = two_rows(sources[xp + i], 4 * t)
                part = dot_nt(lhs, gp[xp, t])
                acc = part if acc is None else acc + part
        for j in range(3):
            slots = []
            for slot in range(4):
                r0 = (j * 4 + slot) * cin
                r1 = ((j + 1) * 4 + slot) * cin
                slots.append(acc[r0 : r0 + cin, : 2 * c1] + acc[r1 : r1 + cin, 2 * c1 :])
            turned = [pltpu.roll(v, c1, 1) for v in slots]
            n = i * 3 + j
            red[n, c2:] = jnp.where(low_half, slots[0], slots[2]) + turned[1]
            lows[n] = slots[2] + turned[3]
            highs[n] = slots[3] + turned[2]
    b1 = bias1[:, : 2 * c1] + bias1[:, 2 * c1 :]
    b1 = b1 + pltpu.roll(b1, c1, 1)
    highs[9] = jnp.concatenate([b1] * (cin // 8), axis=0)
    for m in range(5):
        red[9 + m, c2:] = jnp.where(low_half, lows[2 * m], highs[2 * m + 1])
    hp = pairs // 2
    keep[...] = red[pl.ds(place[1] * hp, hp)]
    send[...] = red[pl.ds((1 - place[1]) * hp, hp)].astype(BF)


def unpack_body(me, *refs):
    pieces, bias, out = refs[:-2], refs[-2], refs[-1]
    nf, _, width = bias.shape
    rows = out.shape[1] // len(pieces)
    swap = swap_majors(rows, nf)
    for s, piece in enumerate(pieces):
        got = dot(swap, piece[: rows * nf]).reshape(nf, rows, width)
        out[:, pl.ds(pl.multiple_of((me[0] ^ s) * rows, rows), rows), :] = got + bias[...]


def finish_body(place, mine, other, g2, b2, g1, b1):
    hp, _, width = mine.shape
    nf, c1 = g2.shape[1], g2.shape[2]
    first = place[1] == 0
    got, more = mine[...], other[...]
    halves = (jnp.where(first, got, more), jnp.where(first, more, got))
    for p in range(2 * hp):
        block = halves[p // hp][p % hp]
        turned = pltpu.roll(block, c1, 1)
        for d, v in zip(block_taps(p), (block, turned)):
            low, high = v[:nf, :c1], v[nf:, :c1]
            if d < 27:
                g2[d] = low
                g1[d] = high
            else:
                column = lax.broadcasted_iota(jnp.int32, low.shape, 0)
                lane = lax.broadcasted_iota(jnp.int32, low.shape, 1)
                row = jnp.sum(jnp.where(column == lane, low, 0.0), axis=0, keepdims=True)
                b2[...] = row[:, :nf]
                b1[...] = high[0:1]


def swap_first(value, axis):
    count = lax.axis_size(axis)
    return lax.ppermute(value, axis, [(i, i ^ 1) for i in range(count)])


def swap_second(value, axis):
    count = lax.axis_size(axis)
    both = lax.axis_size("rep")
    pairs = []
    for i in range(count):
        for r in range(both):
            if i in (0, count - 1):
                pairs.append((i * both + r, i * both + (r ^ 1)))
            else:
                pairs.append((i * both + r, (i + 1 if i % 2 else i - 1) * both + r))
    return lax.ppermute(value, (axis, "rep"), pairs)


def to_partner(value, axis, s):
    count = lax.axis_size(axis)
    return lax.ppermute(value, axis, [(i, i ^ s) for i in range(count)])


def tree_sum(values):
    values = [v.astype(F32) for v in values]
    while len(values) > 1:
        values = [values[n] + values[n + 1] for n in range(0, len(values), 2)]
    return values[0]


def per_device(volume, first_kernel, first_bias, second_kernel, second_bias, cotangent):
    source = volume[0]
    cotan = cotangent[0, :, 0]
    n_sy, n_sx = lax.axis_size("sy"), lax.axis_size("sx")
    sx, sy, rep = (lax.axis_index(a) for a in ("sx", "sy", "rep"))
    odd_x = (sx % 2).astype(jnp.int32)
    odd_y = (sy % 2).astype(jnp.int32)
    cin, planes, rows, width = source.shape
    nf, rows2, width2 = cotan.shape
    c1 = first_kernel.shape[0]
    c2 = nf * n_sy
    own2 = rows // 2
    pairs = 14
    scale = 1.0 / math.sqrt(
        lax.axis_size("rep") * n_sx * n_sy * (planes // 2) * own2 * (width // 2)
    )
    me = sy.astype(jnp.int32).reshape(1)
    place = jnp.stack(
        [
            jnp.asarray(v, jnp.int32)
            for v in (odd_x, rep, (sx > 0) & (sx < n_sx - 1))
        ]
    )
    rim = 1

    w1 = first_kernel.transpose(2, 3, 4, 1, 0)
    w1q = jnp.concatenate(
        [
            jnp.pad(w1, ((0, 0), (0, 0), (0, 1), (0, 0), (0, 0))),
            jnp.pad(w1, ((0, 0), (0, 0), (1, 0), (0, 0), (0, 0))),
        ],
        axis=-1,
    )
    bias4 = jnp.tile(first_bias, 4)[:, None]
    w2 = second_kernel.transpose(2, 3, 4, 0, 1).reshape(27, nf, c1)
    vt = call(
        volume_body,
        "volume_cells",
        jax.ShapeDtypeStruct((planes, rows, cin, width), BF),
        [],
        (source,),
        flops=1 << 30,
    )
    cotan, _ = lax.optimization_barrier((cotan, vt))
    cp, w2p = call(
        prep_body,
        "cotangent_cells",
        [
            jax.ShapeDtypeStruct((n_sy, own2 + 2, nf, width2), BF),
            jax.ShapeDtypeStruct((pairs, nf, 2 * c1), BF),
        ],
        [
            pltpu.VMEM((rows2 + 2, nf, width2), BF),
        ],
        (me, cotan, w2),
        smem_ins=1,
        flops=1 << 30,
    )

    edge_lo, edge_hi = vt[:, :rim], vt[:, rows - rim :]
    ya = swap_first(jnp.where(odd_y == 1, edge_lo, edge_hi), "sy")
    yb = swap_second(jnp.where(odd_y == 1, edge_hi, edge_lo), "sy")
    yb = jnp.where((sy > 0) & (sy < n_sy - 1), yb, jnp.zeros_like(yb))
    rim_lo = jnp.where(odd_y == 1, ya, yb)
    rim_hi = jnp.where(odd_y == 1, yb, ya)
    vr = jnp.concatenate([rim_lo, vt, rim_hi], axis=1)
    za = swap_first(jnp.where(odd_x == 1, vr[0], vr[planes - 1]), "sx")
    zb = swap_second(jnp.where(odd_x == 1, vr[planes - 1], vr[0]), "sx")

    w2_half = lax.dynamic_slice_in_dim(w2p, rep * (pairs // 2), pairs // 2, axis=0)
    both = [
        to_partner(jnp.concatenate([cp[s], w2_half], axis=0), "sy", s) for s in range(1, n_sy)
    ]
    cgot = [cp[0]] + [b[: own2 + 2] for b in both]
    w2_mine = jnp.stack([b[own2 + 2 :] for b in both])
    w2_other = swap_first(w2_mine, "rep")

    pooled_rows = own2
    cell_shape = (rows + 2 * rim, 4 * cin, width // 2)
    cells, w1b, acc = call(
        conv1_own_body,
        "conv1_own",
        [
            jax.ShapeDtypeStruct((planes, *cell_shape), BF),
            jax.ShapeDtypeStruct((3, 4 * c1, 16 * cin), BF),
            jax.ShapeDtypeStruct((2, pooled_rows // 2, 4 * c1, width), F32),
        ],
        [],
        (vr, w1q, bias4),
        flops=2 << 30,
    )
    cgot, acc = lax.optimization_barrier((cgot, acc))
    co = jnp.stack(cgot)
    ca = swap_first(co, "sx")
    cb = swap_second(co, "sx")
    low, high, mask, pooled = call(
        conv1_body,
        "conv1",
        [
            jax.ShapeDtypeStruct(cell_shape, BF),
            jax.ShapeDtypeStruct(cell_shape, BF),
            jax.ShapeDtypeStruct((2, own2, 4 * c1, width // 2), BF),
            jax.ShapeDtypeStruct((pooled_rows, c1, width // 2), BF),
        ],
        [],
        (place, za, zb, w1b, acc),
        smem_ins=1,
        flops=1 << 30,
    )
    w2_other, _ = lax.optimization_barrier((w2_other, pooled))
    w2_first = jnp.where(rep == 0, w2_mine, w2_other)
    w2_second = jnp.where(rep == 0, w2_other, w2_mine)
    w2r = jnp.concatenate(
        [w2p[None], jnp.concatenate([w2_first, w2_second], axis=1)], axis=0
    )
    pa = swap_first(jnp.where(odd_y == 1, pooled[0], pooled[own2 - 1]), "sy")
    pb = swap_second(jnp.where(odd_y == 1, pooled[own2 - 1], pooled[0]), "sy")
    pb = jnp.where((sy > 0) & (sy < n_sy - 1), pb, jnp.zeros_like(pb))
    ur = jnp.concatenate(
        [
            jnp.where(odd_y == 1, pa, pb)[None],
            pooled,
            jnp.where(odd_y == 1, pb, pa)[None],
        ],
        axis=0,
    )
    ua = swap_first(ur, "sx")
    ub = swap_second(ur, "sx")

    plane_shape = (own2 + 2, c2, width2)
    wb, wide, own_back, own_g2, own_b2 = call(
        own_body,
        "backward_own",
        [
            jax.ShapeDtypeStruct((3, 3 * c1, 3 * c2), BF),
            jax.ShapeDtypeStruct((4 * c1, own2 * width2), BF),
            jax.ShapeDtypeStruct((own2 // 2, 3 * c1, 2 * width2), F32),
            jax.ShapeDtypeStruct((3 * c2, 4 * c1), F32),
            jax.ShapeDtypeStruct((c2, 2 * c1), F32),
        ],
        [pltpu.VMEM(plane_shape, BF)],
        (co, pooled, w2r),
        flops=2 << 30,
    )
    hp = pairs // 2
    half_shape = jax.ShapeDtypeStruct((hp, c2 + cin, 2 * c1), F32)
    gp, back_g2, bias1 = call(
        back_body,
        "backward",
        [
            jax.ShapeDtypeStruct((2, own2 // 2, 4 * c1, width), BF),
            jax.ShapeDtypeStruct((2, 3 * c2, 4 * c1), F32),
            jax.ShapeDtypeStruct((8, 4 * c1), F32),
        ],
        [pltpu.VMEM(plane_shape, BF), pltpu.VMEM(plane_shape, BF)],
        (place, mask, wide, ca, cb, wb, own_back),
        smem_ins=1,
        flops=2 << 30,
    )
    keep, send = call(
        weights_body,
        "first_weights",
        [half_shape, jax.ShapeDtypeStruct(half_shape.shape, BF)],
        [pltpu.VMEM((pairs, c2 + cin, 2 * c1), F32)],
        (place, cells, low, high, gp, back_g2, bias1, own_g2, own_b2),
        smem_ins=1,
        flops=3 << 30,
    )

    send, ua, ub = lax.optimization_barrier((send, ua, ub))
    half = keep + swap_first(send, "rep").astype(F32)
    half, ua, ub = lax.optimization_barrier((half, ua, ub))
    half_bf = half.astype(BF)
    tail = half_bf[:, c2:]
    got = [
        to_partner(
            jnp.concatenate([half_bf[:, s * nf : (s + 1) * nf], tail], axis=1), "sy", s
        ).astype(F32)
        for s in range(1, n_sy)
    ]
    pieces = call(
        conv2_body,
        "conv2",
        jax.ShapeDtypeStruct((n_sy, own2, nf, width2), BF),
        [pltpu.VMEM((3, own2 + 2, 3, c1, width2), BF)],
        (place, ur, ua, ub, w2r),
        smem_ins=1,
        flops=1 << 30,
    )
    own = jnp.concatenate([half[:, :nf], tail.astype(F32)], axis=1)
    flat = pieces.reshape(n_sy, own2 * nf, width2)
    beside_sy = to_partner(flat[1], "sy", 1)
    got, beside_sy = lax.optimization_barrier((got, beside_sy))
    part = tree_sum([own] + got).astype(BF)
    part, flat = lax.optimization_barrier((part, flat))
    parts = [part] + [to_partner(part, "sx", s) for s in range(1, n_sx)]
    out_got = [flat[0], beside_sy] + [to_partner(flat[s], "sy", s) for s in range(2, n_sy)]
    bias_wide = jnp.broadcast_to(second_bias[:, None, None], (nf, 1, width2))
    second_out = call(
        unpack_body,
        "unpack",
        jax.ShapeDtypeStruct((nf, rows2, width2), F32),
        [],
        (me, *out_got, bias_wide),
        smem_ins=1,
        flops=1 << 28,
    )
    parts, second_out = lax.optimization_barrier((parts, second_out))
    total = tree_sum(parts) * scale
    other = swap_first(total, "rep")
    g2, t2, g1, t1 = call(
        finish_body,
        "finish",
        [
            jax.ShapeDtypeStruct((27, nf, c1), F32),
            jax.ShapeDtypeStruct((1, nf), F32),
            jax.ShapeDtypeStruct((27, cin, c1), F32),
            jax.ShapeDtypeStruct((1, c1), F32),
        ],
        [],
        (place, total, other),
        smem_ins=1,
        flops=1 << 20,
    )
    return (
        second_out[None, :, None],
        g1.reshape(3, 3, 3, cin, c1).transpose(4, 3, 0, 1, 2),
        t1[0],
        g2.reshape(3, 3, 3, nf, c1).transpose(3, 4, 0, 1, 2),
        t2[0],
    )


def solution(mesh):
    placed = (
        P("rep", None, "sx", "sy", None),
        P(),
        P(),
        P("sy", None, None, None, None),
        P("sy"),
        P("rep", "sy", "sx", None, None),
    )
    return jax.shard_map(
        per_device,
        mesh=mesh,
        in_specs=placed,
        out_specs=(
            P("rep", "sy", "sx", None, None),
            P(),
            P(),
            P("sy", None, None, None, None),
            P("sy"),
        ),
        check_vma=False,
    )
```

```python
import math

import jax
import jax.numpy as jnp
from jax import lax
from jax.experimental import pallas as pl
from jax.experimental.pallas import tpu as pltpu
from jax.sharding import PartitionSpec as P

BF = jnp.bfloat16
F32 = jnp.float32


def dot(a, b):
    return jnp.dot(a, b, preferred_element_type=F32)


def dot_nt(a, b):
    return lax.dot_general(a, b, (((1,), (1,)), ((), ())), preferred_element_type=F32)


def index_pair(rows, cols):
    shape = (rows, cols)
    return (
        lax.broadcasted_iota(jnp.int32, shape, 0),
        lax.broadcasted_iota(jnp.int32, shape, 1),
    )


def one_where(cond):
    return jnp.where(cond, 1.0, 0.0).astype(BF)


def swap_majors(outer, inner):
    r, c = index_pair(outer * inner, outer * inner)
    return one_where(lax.rem(r, outer) * inner + lax.div(r, outer) == c)


def shift_both(width):
    r, c = index_pair(width, 2 * width)
    return one_where(((c < width) & (r == c - 1)) | ((c >= width) & (r == c - width + 1)))


def identity(size):
    r, c = index_pair(size, size)
    return one_where(r == c)


def beside(place, below, first, second):
    use_first = jnp.where((place[0] == 1) == below, 1.0, 0.0)
    use_second = (1.0 - use_first) * jnp.where(place[2] == 1, 1.0, 0.0)
    lanes = (1, first.shape[-1])
    return first[...] * jnp.full(lanes, use_first, F32).astype(BF) + second[...] * jnp.full(
        lanes, use_second, F32
    ).astype(BF)


def call(body, name, outs, scratch, ins, smem_ins=0, flops=0, room=40):
    vm = pl.BlockSpec(memory_space=pltpu.VMEM)
    sm = pl.BlockSpec(memory_space=pltpu.SMEM)
    return pl.pallas_call(
        body,
        name=name,
        out_shape=outs,
        in_specs=[sm] * smem_ins + [vm] * (len(ins) - smem_ins),
        out_specs=jax.tree.map(lambda _: vm, outs),
        scratch_shapes=scratch,
        compiler_params=pltpu.CompilerParams(vmem_limit_bytes=room << 20),
        cost_estimate=pl.CostEstimate(flops=flops, bytes_accessed=1 << 20, transcendentals=0),
    )(*ins)


def volume_body(vol, vt):
    planes, rows, cin, width = vt.shape
    swap = swap_majors(cin, rows)
    half = width // 2
    r, c = index_pair(width, width)
    split = one_where(r == 2 * lax.rem(c, half) + lax.div(c, half))
    for x in range(planes):
        cells = dot(swap, vol[:, x].reshape(cin * rows, width)).astype(BF)
        vt[x] = dot(cells, split).astype(BF).reshape(rows, cin, width)


def prep_body(me, cot, w2, cp, w2p, cpad):
    nf, rows2, width2 = cot.shape
    step = 16
    swap2 = swap_majors(nf, step)
    for h in range(0, rows2, step):
        got = dot(swap2, cot[:, h : h + step].reshape(nf * step, width2))
        cpad[1 + h : 1 + h + step] = got.astype(BF).reshape(step, nf, width2)
    zero = jnp.zeros((1, nf, width2), BF)
    cpad[0:1] = zero
    cpad[rows2 + 1 : rows2 + 2] = zero
    count, rim_rows = cp.shape[0], cp.shape[1]
    for s in range(count):
        cp[s] = cpad[pl.ds((me[0] ^ s) * (rim_rows - 2), rim_rows)]
    taps, _, c1 = w2.shape
    pairs = w2p.shape[0]
    r, c = index_pair(c1, 2 * c1)
    low = dot(w2[:pairs].reshape(pairs * nf, c1), one_where(r == c))
    high = dot(w2[pairs:].reshape((taps - pairs) * nf, c1), one_where(r + c1 == c))
    for p in range(pairs):
        both = low[p * nf : (p + 1) * nf]
        if p + pairs < taps:
            both = both + high[p * nf : (p + 1) * nf]
        w2p[p] = both.astype(BF)


def moved_by_one(width):
    half = width // 2
    r, c = index_pair(width, width)
    return one_where(
        ((c < half) & (c > 0) & (r == half + c - 1))
        | ((c >= half) & (r == c - half + 1) & (r < half))
    )


def fill_cells(cells, plane, moved):
    rows, cin, width = plane.shape
    half = width // 2
    out = dot(plane.reshape(rows * cin, width), moved).astype(BF).reshape(rows, cin, width)
    cells[:, 0:cin] = out[:, :, :half]
    cells[:, cin : 2 * cin] = plane[:, :, :half]
    cells[:, 2 * cin : 3 * cin] = plane[:, :, half:]
    cells[:, 3 * cin : 4 * cin] = out[:, :, half:]


def two_rows(cells, first):
    rows, deep, half = cells.shape
    return jnp.concatenate(
        [cells[first + 2 * n : first + 2 * n + 4].reshape(4 * deep, half) for n in range(2)],
        axis=1,
    )


def conv1_own_body(vr, w1q, bias, cells, w1b, acc):
    planes, rows, cin, width = vr.shape
    c1 = bias.shape[0] // 4
    eye = identity(4 * c1)
    nothing = jnp.zeros((cin, 2 * c1), BF)
    for i in range(3):
        blocks = []
        for ys in range(4):
            for slot in range(4):
                left = w1q[i, ys, slot] if ys < 3 else nothing
                right = w1q[i, ys - 1, slot] if ys > 0 else nothing
                blocks.append(jnp.concatenate([left, right], axis=1))
        w1b[i] = dot_nt(eye, jnp.concatenate(blocks, axis=0)).astype(BF)
    moved = moved_by_one(width)
    for x in range(planes):
        fill_cells(cells.at[x], vr[x], moved)
    for t in range(acc.shape[1]):
        for xp in range(2):
            acc[xp, t] = (
                dot(w1b[1 - xp], two_rows(cells.at[0], 4 * t))
                + dot(w1b[2 - xp], two_rows(cells.at[1], 4 * t))
                + bias[...]
            )


def conv1_body(place, za, zb, w1b, acc, low, high, mask, pooled):
    rows, cin, width = za.shape
    half = width // 2
    c1 = pooled.shape[1]
    moved = moved_by_one(width)
    fill_cells(low, beside(place, True, za, zb), moved)
    fill_cells(high, beside(place, False, za, zb), moved)
    rows2 = pooled.shape[0]
    for t in range(rows2 // 2):
        total = None
        for xp, cells in ((0, low), (1, high)):
            pre = acc[xp, t] + dot(w1b[2 * xp], two_rows(cells, 4 * t))
            above = pre > 0
            flags = jnp.where(above, 1.0, 0.0).astype(BF)
            mask[xp, 2 * t] = flags[:, :half]
            mask[xp, 2 * t + 1] = flags[:, half:]
            act = jnp.where(above, pre, 0.3 * pre)
            for b in range(4):
                piece = act[b * c1 : (b + 1) * c1]
                total = piece if total is None else total + piece
        mean = (total * 0.125).astype(BF)
        pooled[2 * t] = mean[:, :half]
        pooled[2 * t + 1] = mean[:, half:]


def with_shifts(store, plane, shifts):
    rows, chans, width = plane.shape
    out = dot(plane.reshape(rows * chans, width), shifts).astype(BF).reshape(rows, chans, 2 * width)
    store(0, out[:, :, :width])
    store(1, plane)
    store(2, out[:, :, width:])


def conv2_body(place, ur, ua, ub, w2r, pieces, u):
    rows, c1, width = ur.shape
    count, pairs, nf, _ = w2r.shape
    shifts = shift_both(width)
    planes = (beside(place, True, ua, ub), ur[...], beside(place, False, ua, ub))
    for x in range(3):

        def store(k, value, x=x):
            u[x, :, k] = value

        with_shifts(store, planes[x], shifts)
    weights = jnp.concatenate(
        [jnp.concatenate([w2r[s, p] for s in range(count)], axis=0) for p in range(pairs)], axis=1
    )

    def tap(y, d):
        d = d if d < 27 else 0
        return u[d // 9, y + (d // 3) % 3, d % 3]

    def deep(y):
        return jnp.concatenate(
            [tap(y, d) for p in range(pairs) for d in (p, p + pairs)], axis=0
        )

    for y in range(0, rows - 2, 2):
        rhs = jnp.concatenate([deep(y), deep(y + 1)], axis=1)
        out = dot(weights, rhs).astype(BF)
        for s in range(count):
            pieces[s, y] = out[s * nf : (s + 1) * nf, :width]
            pieces[s, y + 1] = out[s * nf : (s + 1) * nf, width:]


def block_taps(block):
    if block < 9:
        return block * 3, block * 3 + 1
    first = 2 * (block - 9)
    return first * 3 + 2, (first + 1) * 3 + 2 if first < 8 else 27


def fill_plane(t_ref, plane):
    for s in range(plane.shape[0]):
        nf = plane.shape[2]
        t_ref[:, s * nf : (s + 1) * nf] = plane[s]


def pair_rows(t_ref, t):
    rows, chans, width = t_ref.shape
    return jnp.concatenate(
        [t_ref[2 * t + n : 2 * t + n + 3].reshape(3 * chans, width) for n in range(2)], axis=1
    )


def rows_wide(t_ref):
    count = t_ref.shape[0] - 2
    return jnp.concatenate(
        [
            jnp.concatenate([t_ref[y + ys] for y in range(count)], axis=1)
            for ys in range(3)
        ],
        axis=0,
    )


def own_body(co, pooled, w2r, wb, wide, own_back, own_g2, own_b2, t_ref):
    count, rows, nf, width = co.shape
    pairs = w2r.shape[1]
    c1 = pooled.shape[1]
    c2 = count * nf
    fill_plane(t_ref, co)
    eye = identity(2 * c1)
    for p in range(pairs):
        block = jnp.concatenate([w2r[s, p] for s in range(count)], axis=0)
        turned = dot_nt(eye, block).astype(BF)
        for half, d in ((0, p), (1, p + pairs)):
            if d < 27:
                i, j, k = d // 9, (d // 3) % 3, d % 3
                at = (2 - j) * c2
                wb[2 - i, k * c1 : (k + 1) * c1, at : at + c2] = turned[
                    half * c1 : (half + 1) * c1
                ]
    for t in range((rows - 2) // 2):
        own_back[t] = dot(wb[1], pair_rows(t_ref, t))
    cells2 = pooled.shape[0]
    moved = dot(pooled[...].reshape(cells2 * c1, width), shift_both(width)).astype(BF)
    for y in range(cells2):
        lanes = slice(y * width, (y + 1) * width)
        after = moved[y * c1 : (y + 1) * c1, width:]
        wide[0:c1, lanes] = moved[y * c1 : (y + 1) * c1, :width]
        wide[c1 : 2 * c1, lanes] = pooled[y]
        wide[2 * c1 : 3 * c1, lanes] = after
        wide[3 * c1 : 4 * c1, lanes] = after
    own_g2[...] = dot_nt(rows_wide(t_ref), wide[...])
    sums = None
    for y in range(1, rows - 1):
        v = t_ref[y].astype(F32)
        sums = v if sums is None else sums + v
    own_b2[...] = jnp.broadcast_to(jnp.sum(sums, axis=1, keepdims=True), own_b2.shape)


def back_body(place, mask, wide, ca, cb, wb, own_back, gp, g2, bias1, t0, t2):
    count, rows, nf, width = ca.shape
    c1 = wide.shape[0] // 4
    fill_plane(t0, beside(place, True, ca, cb))
    fill_plane(t2, beside(place, False, ca, cb))
    sums = jnp.zeros((8, 4 * c1), F32)
    ones = jnp.ones((8, 2 * width), BF)
    lane = lax.broadcasted_iota(jnp.int32, (c1, width), 1)
    for t in range((rows - 2) // 2):
        acc = own_back[t] + dot(wb[0], pair_rows(t0, t)) + dot(wb[2], pair_rows(t2, t))
        rows_back = []
        for n in range(2):
            part = acc[:, n * width : (n + 1) * width]
            ahead = pltpu.roll(part[:c1], width - 1, 1)
            behind = pltpu.roll(part[2 * c1 :], 1, 1)
            rows_back.append(
                part[c1 : 2 * c1]
                + jnp.where(lane < width - 1, ahead, 0.0)
                + jnp.where(lane > 0, behind, 0.0)
            )
        eighth = jnp.concatenate(rows_back, axis=1) * 0.125
        spread = jnp.concatenate([eighth] * 4, axis=0)
        for xp in range(2):
            flags = jnp.concatenate([mask[xp, 2 * t], mask[xp, 2 * t + 1]], axis=1)
            grad = (spread * jnp.where(flags > 0, 1.0, 0.3)).astype(BF)
            gp[xp, t] = grad
            sums = sums + dot_nt(ones, grad)
    bias1[...] = sums
    g2[0] = dot_nt(rows_wide(t0), wide[...])
    g2[1] = dot_nt(rows_wide(t2), wide[...])


def weights_body(place, cells, low, high, gp, g2, bias1, own_g2, own_b2, keep, send, red):
    c2, wide_lanes = own_b2.shape
    c1 = wide_lanes // 2
    cin = cells.shape[2] // 4
    n_pairs = gp.shape[1]
    pairs = 14
    sources = (low, cells.at[0], cells.at[1], high)

    def part2(ij):
        x, ys = 2 - ij // 3, 2 - ij % 3
        rows_of = slice(ys * c2, (ys + 1) * c2)
        return own_g2[rows_of] if x == 1 else g2[x // 2, rows_of]

    low_wide = lax.broadcasted_iota(jnp.int32, (c2, 2 * c1), 1) < c1
    for ij in range(9):
        red[ij, :c2] = part2(ij)[:, : 2 * c1]
    for m in range(5):
        other = part2(2 * m + 1)[:, 2 * c1 :] if m < 4 else own_b2[...]
        red[9 + m, :c2] = jnp.where(low_wide, part2(2 * m)[:, 2 * c1 :], other)
    lane = lax.broadcasted_iota(jnp.int32, (cin, 2 * c1), 1)
    low_half = lane < c1
    lows, highs = {}, {}
    for i in range(3):
        acc = None
        for xp in range(2):
            for t in range(n_pairs):
                lhs = two_rows(sources[xp + i], 4 * t)
                part = dot_nt(lhs, gp[xp, t])
                acc = part if acc is None else acc + part
        for j in range(3):
            slots = []
            for slot in range(4):
                r0 = (j * 4 + slot) * cin
                r1 = ((j + 1) * 4 + slot) * cin
                slots.append(acc[r0 : r0 + cin, : 2 * c1] + acc[r1 : r1 + cin, 2 * c1 :])
            turned = [pltpu.roll(v, c1, 1) for v in slots]
            n = i * 3 + j
            red[n, c2:] = jnp.where(low_half, slots[0], slots[2]) + turned[1]
            lows[n] = slots[2] + turned[3]
            highs[n] = slots[3] + turned[2]
    b1 = bias1[:, : 2 * c1] + bias1[:, 2 * c1 :]
    b1 = b1 + pltpu.roll(b1, c1, 1)
    highs[9] = jnp.concatenate([b1] * (cin // 8), axis=0)
    for m in range(5):
        red[9 + m, c2:] = jnp.where(low_half, lows[2 * m], highs[2 * m + 1])
    hp = pairs // 2
    keep[...] = red[pl.ds(place[1] * hp, hp)]
    send[...] = red[pl.ds((1 - place[1]) * hp, hp)].astype(BF)


def unpack_body(me, *refs):
    pieces, bias, out = refs[:-2], refs[-2], refs[-1]
    nf, _, width = bias.shape
    rows = out.shape[1] // len(pieces)
    swap = swap_majors(rows, nf)
    for s, piece in enumerate(pieces):
        got = dot(swap, piece[: rows * nf]).reshape(nf, rows, width)
        out[:, pl.ds(pl.multiple_of((me[0] ^ s) * rows, rows), rows), :] = got + bias[...]


def finish_body(place, mine, other, g2, b2, g1, b1):
    hp, _, width = mine.shape
    nf, c1 = g2.shape[1], g2.shape[2]
    first = place[1] == 0
    got, more = mine[...], other[...]
    halves = (jnp.where(first, got, more), jnp.where(first, more, got))
    for p in range(2 * hp):
        block = halves[p // hp][p % hp]
        turned = pltpu.roll(block, c1, 1)
        for d, v in zip(block_taps(p), (block, turned)):
            low, high = v[:nf, :c1], v[nf:, :c1]
            if d < 27:
                g2[d] = low
                g1[d] = high
            else:
                column = lax.broadcasted_iota(jnp.int32, low.shape, 0)
                lane = lax.broadcasted_iota(jnp.int32, low.shape, 1)
                row = jnp.sum(jnp.where(column == lane, low, 0.0), axis=0, keepdims=True)
                b2[...] = row[:, :nf]
                b1[...] = high[0:1]


def swap_first(value, axis):
    count = lax.axis_size(axis)
    return lax.ppermute(value, axis, [(i, i ^ 1) for i in range(count)])


def swap_second(value, axis):
    count = lax.axis_size(axis)
    both = lax.axis_size("rep")
    pairs = []
    for i in range(count):
        for r in range(both):
            if i in (0, count - 1):
                pairs.append((i * both + r, i * both + (r ^ 1)))
            else:
                pairs.append((i * both + r, (i + 1 if i % 2 else i - 1) * both + r))
    return lax.ppermute(value, (axis, "rep"), pairs)


def to_partner(value, axis, s):
    count = lax.axis_size(axis)
    return lax.ppermute(value, axis, [(i, i ^ s) for i in range(count)])


def tree_sum(values):
    values = [v.astype(F32) for v in values]
    while len(values) > 1:
        values = [values[n] + values[n + 1] for n in range(0, len(values), 2)]
    return values[0]


def per_device(volume, first_kernel, first_bias, second_kernel, second_bias, cotangent):
    source = volume[0]
    cotan = cotangent[0, :, 0]
    n_sy, n_sx = lax.axis_size("sy"), lax.axis_size("sx")
    sx, sy, rep = (lax.axis_index(a) for a in ("sx", "sy", "rep"))
    odd_x = (sx % 2).astype(jnp.int32)
    odd_y = (sy % 2).astype(jnp.int32)
    cin, planes, rows, width = source.shape
    nf, rows2, width2 = cotan.shape
    c1 = first_kernel.shape[0]
    c2 = nf * n_sy
    own2 = rows // 2
    pairs = 14
    scale = 1.0 / math.sqrt(
        lax.axis_size("rep") * n_sx * n_sy * (planes // 2) * own2 * (width // 2)
    )
    me = sy.astype(jnp.int32).reshape(1)
    place = jnp.stack(
        [
            jnp.asarray(v, jnp.int32)
            for v in (odd_x, rep, (sx > 0) & (sx < n_sx - 1))
        ]
    )
    rim = 1

    w1 = first_kernel.transpose(2, 3, 4, 1, 0)
    w1q = jnp.concatenate(
        [
            jnp.pad(w1, ((0, 0), (0, 0), (0, 1), (0, 0), (0, 0))),
            jnp.pad(w1, ((0, 0), (0, 0), (1, 0), (0, 0), (0, 0))),
        ],
        axis=-1,
    )
    bias4 = jnp.tile(first_bias, 4)[:, None]
    w2 = second_kernel.transpose(2, 3, 4, 0, 1).reshape(27, nf, c1)
    vt = call(
        volume_body,
        "volume_cells",
        jax.ShapeDtypeStruct((planes, rows, cin, width), BF),
        [],
        (source,),
        flops=1 << 30,
    )
    cotan, _ = lax.optimization_barrier((cotan, vt))
    cp, w2p = call(
        prep_body,
        "cotangent_cells",
        [
            jax.ShapeDtypeStruct((n_sy, own2 + 2, nf, width2), BF),
            jax.ShapeDtypeStruct((pairs, nf, 2 * c1), BF),
        ],
        [
            pltpu.VMEM((rows2 + 2, nf, width2), BF),
        ],
        (me, cotan, w2),
        smem_ins=1,
        flops=1 << 30,
    )

    edge_lo, edge_hi = vt[:, :rim], vt[:, rows - rim :]
    ya = swap_first(jnp.where(odd_y == 1, edge_lo, edge_hi), "sy")
    yb = swap_second(jnp.where(odd_y == 1, edge_hi, edge_lo), "sy")
    yb = jnp.where((sy > 0) & (sy < n_sy - 1), yb, jnp.zeros_like(yb))
    rim_lo = jnp.where(odd_y == 1, ya, yb)
    rim_hi = jnp.where(odd_y == 1, yb, ya)
    vr = jnp.concatenate([rim_lo, vt, rim_hi], axis=1)
    za = swap_first(jnp.where(odd_x == 1, vr[0], vr[planes - 1]), "sx")
    zb = swap_second(jnp.where(odd_x == 1, vr[planes - 1], vr[0]), "sx")

    w2_half = lax.dynamic_slice_in_dim(w2p, rep * (pairs // 2), pairs // 2, axis=0)
    both = [
        to_partner(jnp.concatenate([cp[s], w2_half], axis=0), "sy", s) for s in range(1, n_sy)
    ]
    cgot = [cp[0]] + [b[: own2 + 2] for b in both]
    w2_mine = jnp.stack([b[own2 + 2 :] for b in both])
    w2_other = swap_first(w2_mine, "rep")

    pooled_rows = own2
    cell_shape = (rows + 2 * rim, 4 * cin, width // 2)
    cells, w1b, acc = call(
        conv1_own_body,
        "conv1_own",
        [
            jax.ShapeDtypeStruct((planes, *cell_shape), BF),
            jax.ShapeDtypeStruct((3, 4 * c1, 16 * cin), BF),
            jax.ShapeDtypeStruct((2, pooled_rows // 2, 4 * c1, width), F32),
        ],
        [],
        (vr, w1q, bias4),
        flops=2 << 30,
    )
    cgot, acc = lax.optimization_barrier((cgot, acc))
    co = jnp.stack(cgot)
    ca = swap_first(co, "sx")
    cb = swap_second(co, "sx")
    low, high, mask, pooled = call(
        conv1_body,
        "conv1",
        [
            jax.ShapeDtypeStruct(cell_shape, BF),
            jax.ShapeDtypeStruct(cell_shape, BF),
            jax.ShapeDtypeStruct((2, own2, 4 * c1, width // 2), BF),
            jax.ShapeDtypeStruct((pooled_rows, c1, width // 2), BF),
        ],
        [],
        (place, za, zb, w1b, acc),
        smem_ins=1,
        flops=1 << 30,
    )
    w2_other, _ = lax.optimization_barrier((w2_other, pooled))
    w2_first = jnp.where(rep == 0, w2_mine, w2_other)
    w2_second = jnp.where(rep == 0, w2_other, w2_mine)
    w2r = jnp.concatenate(
        [w2p[None], jnp.concatenate([w2_first, w2_second], axis=1)], axis=0
    )
    pa = swap_first(jnp.where(odd_y == 1, pooled[0], pooled[own2 - 1]), "sy")
    pb = swap_second(jnp.where(odd_y == 1, pooled[own2 - 1], pooled[0]), "sy")
    pb = jnp.where((sy > 0) & (sy < n_sy - 1), pb, jnp.zeros_like(pb))
    ur = jnp.concatenate(
        [
            jnp.where(odd_y == 1, pa, pb)[None],
            pooled,
            jnp.where(odd_y == 1, pb, pa)[None],
        ],
        axis=0,
    )
    ua = swap_first(ur, "sx")
    ub = swap_second(ur, "sx")

    plane_shape = (own2 + 2, c2, width2)
    wb, wide, own_back, own_g2, own_b2 = call(
        own_body,
        "backward_own",
        [
            jax.ShapeDtypeStruct((3, 3 * c1, 3 * c2), BF),
            jax.ShapeDtypeStruct((4 * c1, own2 * width2), BF),
            jax.ShapeDtypeStruct((own2 // 2, 3 * c1, 2 * width2), F32),
            jax.ShapeDtypeStruct((3 * c2, 4 * c1), F32),
            jax.ShapeDtypeStruct((c2, 2 * c1), F32),
        ],
        [pltpu.VMEM(plane_shape, BF)],
        (co, pooled, w2r),
        flops=2 << 30,
    )
    hp = pairs // 2
    half_shape = jax.ShapeDtypeStruct((hp, c2 + cin, 2 * c1), F32)
    gp, back_g2, bias1 = call(
        back_body,
        "backward",
        [
            jax.ShapeDtypeStruct((2, own2 // 2, 4 * c1, width), BF),
            jax.ShapeDtypeStruct((2, 3 * c2, 4 * c1), F32),
            jax.ShapeDtypeStruct((8, 4 * c1), F32),
        ],
        [pltpu.VMEM(plane_shape, BF), pltpu.VMEM(plane_shape, BF)],
        (place, mask, wide, ca, cb, wb, own_back),
        smem_ins=1,
        flops=2 << 30,
    )
    keep, send = call(
        weights_body,
        "first_weights",
        [half_shape, jax.ShapeDtypeStruct(half_shape.shape, BF)],
        [pltpu.VMEM((pairs, c2 + cin, 2 * c1), F32)],
        (place, cells, low, high, gp, back_g2, bias1, own_g2, own_b2),
        smem_ins=1,
        flops=3 << 30,
    )

    send, ua, ub = lax.optimization_barrier((send, ua, ub))
    half = keep + swap_first(send, "rep").astype(F32)
    half, ua, ub = lax.optimization_barrier((half, ua, ub))
    half_bf = half.astype(BF)
    tail = half_bf[:, c2:]
    got = [
        to_partner(
            jnp.concatenate([half_bf[:, s * nf : (s + 1) * nf], tail], axis=1), "sy", s
        ).astype(F32)
        for s in range(1, n_sy)
    ]
    pieces = call(
        conv2_body,
        "conv2",
        jax.ShapeDtypeStruct((n_sy, own2, nf, width2), BF),
        [pltpu.VMEM((3, own2 + 2, 3, c1, width2), BF)],
        (place, ur, ua, ub, w2r),
        smem_ins=1,
        flops=1 << 30,
    )
    own = jnp.concatenate([half[:, :nf], tail.astype(F32)], axis=1)
    flat = pieces.reshape(n_sy, own2 * nf, width2)
    beside_sy = to_partner(flat[1], "sy", 1)
    got, beside_sy = lax.optimization_barrier((got, beside_sy))
    part = tree_sum([own] + got).astype(BF)
    part, flat = lax.optimization_barrier((part, flat))
    parts = [part] + [to_partner(part, "sx", s) for s in range(1, n_sx)]
    out_got = [flat[0], beside_sy] + [to_partner(flat[s], "sy", s) for s in range(2, n_sy)]
    parts, out_got = lax.optimization_barrier((parts, out_got))
    bias_wide = jnp.broadcast_to(second_bias[:, None, None], (nf, 1, width2))
    second_out = call(
        unpack_body,
        "unpack",
        jax.ShapeDtypeStruct((nf, rows2, width2), F32),
        [],
        (me, *out_got, bias_wide),
        smem_ins=1,
        flops=1 << 28,
    )
    total = tree_sum(parts) * scale
    other = swap_first(total, "rep")
    other, second_out = lax.optimization_barrier((other, second_out))
    g2, t2, g1, t1 = call(
        finish_body,
        "finish",
        [
            jax.ShapeDtypeStruct((27, nf, c1), F32),
            jax.ShapeDtypeStruct((1, nf), F32),
            jax.ShapeDtypeStruct((27, cin, c1), F32),
            jax.ShapeDtypeStruct((1, c1), F32),
        ],
        [],
        (place, total, other),
        smem_ins=1,
        flops=1 << 20,
    )
    return (
        second_out[None, :, None],
        g1.reshape(3, 3, 3, cin, c1).transpose(4, 3, 0, 1, 2),
        t1[0],
        g2.reshape(3, 3, 3, nf, c1).transpose(3, 4, 0, 1, 2),
        t2[0],
    )


def solution(mesh):
    placed = (
        P("rep", None, "sx", "sy", None),
        P(),
        P(),
        P("sy", None, None, None, None),
        P("sy"),
        P("rep", "sy", "sx", None, None),
    )
    return jax.shard_map(
        per_device,
        mesh=mesh,
        in_specs=placed,
        out_specs=(
            P("rep", "sy", "sx", None, None),
            P(),
            P(),
            P("sy", None, None, None, None),
            P("sy"),
        ),
        check_vma=False,
    )
```
